128 devices in a mesh: row: 16 (over y_lo, z, core), col: 8 (over y_hi, x).
Axes of the slice: x: 4, y: 4 (y_hi: 2, y_lo: 2; y = y_hi * 2 + y_lo), z: 4, core: 2. Of those that a mesh axis runs over, the one named last changes fastest.
Arguments:
- tokens: bfloat16 [1024, 6144], P('col', 'row'), may hold values from -6 to 6
- weight_in: bfloat16 [6144, 24576], P('row', 'col'), may hold values from -0.078125 to 0.078125
- weight_out: bfloat16 [24576, 6144], P('col', 'row'), may hold values from -0.078125 to 0.078125
- upstream: bfloat16 [1024, 6144], P('col', 'row'), may hold values from -6 to 6
Outputs:
- grad_tokens: bfloat16 [1024, 6144], P('col', 'row')
- grad_in: bfloat16 [6144, 24576], P('row', 'col')
- grad_out: bfloat16 [24576, 6144], P('col', 'row')
The draws below stay inside these ranges and needn't reach their ends.
All inputs are finite; a program needn't handle non-finite values.
Results may differ from the reference program's by a relative error of at most 0.005.
Values may be sent and summed in bfloat16 or wider, within the bound.
A program may use at most 128 MiB of HBM per device.

```python
import jax
import jax.numpy as jnp
from jax import lax

D = 6144
FF = 24576
TOKENS = 1024


def with_spikes(entries, rng, source, target, shards_of, factor):
    owner, partner = [(jnp.arange(entries.shape[position]) // (entries.shape[position] // shards_of)).reshape([-1 if axis == position else 1 for axis in range(entries.ndim)]) for position in (source, target)]
    chosen = jax.random.permutation(rng, shards_of)[partner]
    strong = (owner == chosen) | (owner == (partner + shards_of // 2) % shards_of)
    return jnp.where(strong, factor * entries, entries)


def shard_levels(own_key, dims, split, least, top_value):
    def one(position, blocks):
        draws = jax.random.uniform(jax.random.fold_in(jax.random.fold_in(own_key, 6), position), (blocks,), jnp.float32, least / len(split), top_value / len(split))
        return jnp.repeat(jnp.exp(draws), dims[position] // blocks).reshape((-1,) + (1,) * (len(dims) - position - 1))

    gain = one(*split[0])
    for cut in split[1:]:
        gain = gain * one(*cut)
    return gain


def noise(own_key, shape, deviation, limit, pieces=(), kind=jnp.bfloat16):
    drawn = deviation * jax.random.normal(own_key, shape, jnp.float32)
    if pieces:
        drawn = drawn * shard_levels(own_key, shape, pieces, -0.22, 0.18)
    return jnp.clip(drawn, -limit, limit).astype(kind)


def noise_with(stream_key, dims, spread, most, shards, heavy, held_as=jnp.bfloat16):
    drawn = spread * jax.random.normal(stream_key, dims, jnp.float32)
    if shards:
        drawn = drawn * shard_levels(stream_key, dims, shards, -0.22, 0.18)
    return jnp.clip(with_spikes(drawn, jax.random.fold_in(stream_key, 3), *heavy), -most, most).astype(held_as)


def setup_inputs(seed: int = 0) -> dict:
    seeds = jax.random.split(jax.random.key(seed), 5)
    tokens = noise_with(seeds[0], (TOKENS, D), 1.0, 6.0, ((0, 8), (1, 16)), (1, 0, 16, 2.0))
    weight_in = noise(seeds[1], (D, FF), D ** -0.5, 0.078125, ((0, 16), (1, 8)))
    weight_out = noise(seeds[2], (FF, D), D ** -0.5, 0.078125, ((0, 8), (1, 16)))
    upstream = noise_with(seeds[3], (TOKENS, D), 1.0, 6.0, ((0, 8), (1, 16)), (1, 0, 16, 2.0))
    return dict(tokens=tokens, weight_in=weight_in, weight_out=weight_out, upstream=upstream)


coef = 0.7978845608
cubic = 0.044715


def gelu_pair(hidden):
    inner = coef * (hidden + cubic * hidden * hidden * hidden)
    tangent = jnp.tanh(inner)
    value = 0.5 * hidden * (1.0 + tangent)
    slope = 0.5 * (1.0 + tangent) + 0.5 * hidden * (1.0 - tangent * tangent) * coef * (1.0 + 3.0 * cubic * hidden * hidden)
    return value, slope


def reference(tokens, weight_in, weight_out, upstream):
    hidden = jnp.dot(tokens, weight_in, preferred_element_type=jnp.float32)
    back = lax.dot_general(upstream, weight_out, (((1,), (1,)), ((), ())), preferred_element_type=jnp.float32)
    value, slope = gelu_pair(hidden)
    act = value.astype(jnp.bfloat16)
    hidden_grad = (back * slope).astype(jnp.bfloat16)
    grad_tokens = lax.dot_general(hidden_grad, weight_in, (((1,), (1,)), ((), ())), preferred_element_type=jnp.float32).astype(jnp.bfloat16)
    grad_in = lax.dot_general(tokens, hidden_grad, (((0,), (0,)), ((), ())), preferred_element_type=jnp.float32).astype(jnp.bfloat16)
    grad_out = lax.dot_general(act, upstream, (((0,), (0,)), ((), ())), preferred_element_type=jnp.float32).astype(jnp.bfloat16)
    return grad_tokens, grad_in, grad_out
```

```python
import jax
import jax.numpy as jnp
from jax import lax
from jax.experimental import pallas as pl
from jax.experimental.pallas import tpu as pltpu
from jax.sharding import PartitionSpec as P

coef = 0.7978845608
cubic = 0.044715
BF = jnp.bfloat16
F32 = jnp.float32
MESH = pl.DeviceIdType.MESH

N = 8
TB = 128
DH = 384
DC = 768
FH = 1536
FP = 512
FQ = 1024
TILE = 512


def activate(hidden, back):
    inner = coef * (hidden + cubic * hidden * hidden * hidden)
    tangent = jnp.tanh(inner)
    value = 0.5 * hidden * (1.0 + tangent)
    slope = 0.5 * (1.0 + tangent) + 0.5 * hidden * (1.0 - tangent * tangent) * coef * (
        1.0 + 3.0 * cubic * hidden * hidden
    )
    return value.astype(BF), (back * slope).astype(BF)


def dot(left, right):
    return jnp.dot(left, right, preferred_element_type=F32)


def dot_nt(left, right):
    return lax.dot_general(
        left, right, (((1,), (1,)), ((), ())), preferred_element_type=F32
    )


def kernel(
    tok_ref, win_ref, wout_ref, up_ref,
    gtok_ref, gin_ref, gout_ref,
    wi, wo, tk, pp, yp, s1, rzp, szp, gp, pq, rzq, szq, kq, syq, yq, gq,
    acci, acco, sti, sto, down, doth, dsib, dr, yhs, yhr, tkt,
    ss, rs, ls, ws, wr, os, orr, hs, hr,
):
    r, c = lax.axis_index("row"), lax.axis_index("col")
    yl, z, k = r // 8, (r // 2) % 4, r % 2
    yh, x = c // 4, c % 4
    zr, zl, z2 = (z + 1) % 4, (z + 3) % 4, (z + 2) % 4

    def at_row(yl_, z_, k_):
        return (yl_ * 8 + z_ * 2 + k_, c)

    def at_col(yh_, x_):
        return (r, yh_ * 4 + x_)

    sib, ypart = at_row(yl, z, 1 - k), at_row(1 - yl, z, k)
    right, left = at_row(yl, zr, k), at_row(yl, zl, k)
    yhp = at_col(1 - yh, x)
    xr, xl, xx = at_col(yh, (x + 1) % 4), at_col(yh, (x + 3) % 4), at_col(yh, (x + 2) % 4)

    def rc(src, dst, send, recv, dev):
        return pltpu.make_async_remote_copy(
            src_ref=src, dst_ref=dst, send_sem=send, recv_sem=recv,
            device_id=dev, device_id_type=MESH,
        )

    def rows(i, size):
        return pl.ds(pl.multiple_of(i * size, size), size)

    def msg(n, i):
        own_p = pl.ds(pl.multiple_of(yl * 64 + z * 16, 16), 16)
        left_p = pl.ds(pl.multiple_of(yl * 64 + zl * 16, 16), 16)
        right_p = pl.ds(pl.multiple_of(yl * 64 + zr * 16, 16), 16)
        own_q = pl.ds(pl.multiple_of(z * 32 + yl * 16, 16), 16)
        if i == 0:
            src, dst, dev = pp.at[n, :, rows(1 - yl, 64)], yp.at[n], ypart
        elif i == 1:
            src, dst, dev = s1.at[n, 0, rows(z2, 16)], rzp.at[n, 0], right
        elif i == 2:
            src, dst, dev = s1.at[n, 1, rows(zr, 16)], rzp.at[n, 1], right
        elif i == 3:
            src, dst, dev = s1.at[n, 1, rows(z2, 16)], rzp.at[n, 2], left
        elif i == 4:
            src, dst, dev = s1.at[n, 0, rows(zl, 16)], rzp.at[n, 3], left
        elif i == 5:
            src, dst, dev = szp.at[n, 0], rzp.at[n, 4], right
        elif i == 6:
            src, dst, dev = szp.at[n, 1], rzp.at[n, 5], left
        elif i in (7, 8):
            src = dst = gp.at[n, :, own_p]
            dev = right if i == 7 else left
        elif i == 9:
            src = dst = gp.at[n, 0, left_p]
            dev = right
        elif i == 10:
            src = dst = gp.at[n, 1, right_p]
            dev = left
        elif i == 11:
            src = dst = gp.at[n, :, rows(yl, 64)]
            dev = ypart
        elif i == 12:
            src, dst, dev = syq.at[n], yq.at[n], ypart
        elif i == 13:
            src, dst, dev = pq.at[n, 0, rows(z2, 32)], rzq.at[n, 0], right
        elif i == 14:
            src, dst, dev = pq.at[n, 1, rows(zr, 32)], rzq.at[n, 1], right
        elif i == 15:
            src, dst, dev = pq.at[n, 1, rows(z2, 32)], rzq.at[n, 2], left
        elif i == 16:
            src, dst, dev = pq.at[n, 0, rows(zl, 32)], rzq.at[n, 3], left
        elif i == 17:
            src, dst, dev = szq.at[n, 0], rzq.at[n, 4], right
        elif i == 18:
            src, dst, dev = szq.at[n, 1], rzq.at[n, 5], left
        elif i == 19:
            src = dst = gq.at[n, :, own_q]
            dev = ypart
        elif i in (20, 21):
            src = dst = gq.at[n, :, rows(z, 32)]
            dev = right if i == 20 else left
        elif i == 22:
            src = dst = gq.at[n, 0, rows(zl, 32)]
            dev = right
        elif i == 23:
            src = dst = gq.at[n, 1, rows(zr, 32)]
            dev = left
        elif i == 24:
            src, dst, dev = doth.at[n], dsib.at[n], sib
        elif i == 25:
            m = (n + 2) % 3
            dx = 1 + 2 * m - 3 * (m // 2)
            src, dst, dev = down.at[n], dr.at[n], at_col(yh, (x + dx) % 4)
        elif i == 27:
            src = dst = tk.at[n, :, :, own_d]
            dev = sib
        return rc(src, dst, ss.at[n, i], rs.at[n, i], dev)

    own_d = pl.ds(pl.multiple_of(k * DH, DH), DH)
    oth_d = pl.ds(pl.multiple_of((1 - k) * DH, DH), DH)
    own_f = pl.ds(pl.multiple_of(k * FH, FH), FH)
    oth_f = pl.ds(pl.multiple_of((1 - k) * FH, FH), FH)

    def tok_msg(m):
        dev = {1: xl, 2: xr, 3: xx, 4: xl, 5: xr, 6: xx, 7: yhp}[m]
        src = tk.at[0 if m in (1, 2, 3, 7) else 7, :, :, own_d]
        return rc(src, tk.at[m, :, :, own_d], ss.at[m, 26], rs.at[m, 26], dev)

    w_out = [
        rc(win_ref.at[:, oth_f], wi.at[own_d], ws.at[0], wr.at[0], sib),
        rc(wout_ref.at[oth_f], wo.at[:, own_d], ws.at[1], wr.at[1], sib),
    ]
    w_own = [
        pltpu.make_async_copy(win_ref.at[:, own_f], wi.at[own_d], ls.at[0]),
        pltpu.make_async_copy(wout_ref.at[own_f], wo.at[:, own_d], ls.at[1]),
    ]
    for cp in w_own:
        cp.start()
    tk[0, 0, :, own_d] = tok_ref[...]
    tk[0, 1, :, own_d] = up_ref[...]

    barrier = pltpu.get_barrier_semaphore()
    partners = (sib, ypart, right, left, yhp, xr, xl, xx)
    for dev in partners:
        pl.semaphore_signal(barrier, inc=1, device_id=dev, device_id_type=MESH)
    pl.semaphore_wait(barrier, len(partners))

    msg(0, 27).start()
    tok_msg(7).start()
    for cp in w_out:
        cp.start()
    for m in (1, 2, 3):
        tok_msg(m).start()
    acci[...] = jnp.zeros_like(acci)
    acco[...] = jnp.zeros_like(acco)
    for cp in w_own:
        cp.wait()
    for cp in w_out:
        cp.wait_recv()

    def s0(n):
        msg(n, 27).wait_recv()
        pp[n, 0] = dot(tk[n, 0], wi[:, 0:FP]).astype(BF)
        pp[n, 1] = dot_nt(tk[n, 1], wo[0:FP, :]).astype(BF)
        msg(n, 0).start()
        for j in range(0, FQ, TILE):
            pq[n, 0, :, j : j + TILE] = dot(tk[n, 0], wi[:, FP + j : FP + j + TILE]).astype(BF)
            pq[n, 1, :, j : j + TILE] = dot_nt(tk[n, 1], wo[FP + j : FP + j + TILE, :]).astype(BF)
        for i in (13, 15, 14, 16):
            msg(n, i).start()

    def s1f(n):
        msg(n, 0).wait_recv()
        s1[n] = (pp[n, :, rows(yl, 64)].astype(F32) + yp[n].astype(F32)).astype(BF)
        for i in (1, 3, 2, 4):
            msg(n, i).start()
        msg(n, 13).wait_recv()
        szq[n, 0] = (pq[n, 0, rows(zr, 32)].astype(F32) + rzq[n, 0].astype(F32)).astype(BF)
        msg(n, 17).start()
        msg(n, 15).wait_recv()
        szq[n, 1] = (pq[n, 1, rows(zl, 32)].astype(F32) + rzq[n, 2].astype(F32)).astype(BF)
        msg(n, 18).start()

    def s2(n):
        msg(n, 1).wait_recv()
        szp[n, 0] = (s1[n, 0, rows(zr, 16)].astype(F32) + rzp[n, 0].astype(F32)).astype(BF)
        msg(n, 5).start()
        msg(n, 3).wait_recv()
        szp[n, 1] = (s1[n, 1, rows(zl, 16)].astype(F32) + rzp[n, 2].astype(F32)).astype(BF)
        msg(n, 6).start()
        for i in (14, 16, 17, 18):
            msg(n, i).wait_recv()
        for t, a, b in ((0, 3, 4), (1, 1, 5)):
            for mine in (False, True):
                half = yl if mine else 1 - yl
                here = pl.ds(pl.multiple_of(z * 32 + half * 16, 16), 16)
                total = (
                    pq[n, t, here].astype(F32)
                    + rzq[n, a, rows(half, 16)].astype(F32)
                    + rzq[n, b, rows(half, 16)].astype(F32)
                )
                if mine:
                    kq[n, t] = total
                else:
                    syq[n, t] = total.astype(BF)
        msg(n, 12).start()

    def s3(n):
        for i in (2, 4, 5, 6):
            msg(n, i).wait_recv()
        hidden = s1[n, 0, rows(z, 16)].astype(F32) + rzp[n, 3].astype(F32) + rzp[n, 4].astype(F32)
        back = s1[n, 1, rows(z, 16)].astype(F32) + rzp[n, 1].astype(F32) + rzp[n, 5].astype(F32)
        here = pl.ds(pl.multiple_of(yl * 64 + z * 16, 16), 16)
        gp[n, 0, here], gp[n, 1, here] = activate(hidden, back)
        msg(n, 7).start()
        msg(n, 8).start()
        msg(n, 12).wait_recv()
        here = pl.ds(pl.multiple_of(z * 32 + yl * 16, 16), 16)
        gq[n, 0, here], gq[n, 1, here] = activate(
            kq[n, 0] + yq[n, 0].astype(F32), kq[n, 1] + yq[n, 1].astype(F32)
        )
        msg(n, 19).start()

    def s4(n):
        msg(n, 19).wait_recv()
        msg(n, 20).start()
        msg(n, 21).start()
        msg(n, 7).wait_recv()
        msg(n, 9).start()
        msg(n, 8).wait_recv()
        msg(n, 10).start()

    def s5(n):
        msg(n, 9).wait_recv()
        msg(n, 10).wait_recv()
        msg(n, 11).start()
        msg(n, 20).wait_recv()
        msg(n, 22).start()
        msg(n, 21).wait_recv()
        msg(n, 23).start()

    def s6_wait(n):
        for i in (11, 22, 23):
            msg(n, i).wait_recv()

    def cols(t, n):
        ref = gp
        yield 0, ref[n, t]
        for j in range(0, FQ, TILE):
            yield FP + j, gq[n, t, :, j : j + TILE]

    def s6a(n):
        tkt[...] = tk[n, 0].T
        for j, g in cols(1, n):
            acci[:, j : j + TILE] += dot(tkt[...], g)

    def s6b(n):
        for half, ref in ((oth_d, doth), (own_d, down)):
            ref[n] = dot_nt(gp[n, 1], wi[half, 0:FP]) + dot_nt(gq[n, 1], wi[half, FP:FH])
            if ref is doth:
                msg(n, 24).start()
        for j, a in cols(0, n):
            acco[j : j + TILE, :] += dot(a.T, tk[n, 1])

    def s7(n):
        msg(n, 24).wait_recv()
        down[n] += dsib[n]

    def step(n, _):
        @pl.when(n >= 1)
        def _():
            s3(n - 1)

        @pl.when(n < N)
        def _():
            s0(n)
            s1f(n)

        @pl.when(n >= 1)
        def _():
            s4(n - 1)

        @pl.when(n == 0)
        def _():
            tok_msg(7).wait_recv()
            for m in (4, 5, 6):
                tok_msg(m).start()
            msg(7, 27).start()

        for m in range(1, 7):

            @pl.when(n == m - 1)
            def _():
                tok_msg(m).wait_recv()
                msg(m, 27).start()

        @pl.when(n >= 2)
        def _():
            s6_wait(n - 2)
            s6a(n - 2)

        @pl.when(n < N)
        def _():
            s2(n)

        @pl.when(n >= 1)
        def _():
            s5(n - 1)

        @pl.when(n >= 2)
        def _():
            s6b(n - 2)

        @pl.when(n >= 3)
        def _():
            s7(n - 3)

        @pl.when(n >= 4)
        def _():
            msg(n - 3, 25).start()

        return 0

    lax.fori_loop(0, N + 1, step, 0)

    last = N - 1
    s6_wait(last)
    for half, ref in ((oth_d, doth), (own_d, down)):
        ref[last] = dot_nt(gp[last, 1], wi[half, 0:FP]) + dot_nt(gq[last, 1], wi[half, FP:FH])
        if ref is doth:
            msg(last, 24).start()
    s7(last - 1)
    msg(last - 1, 25).start()
    tkt[...] = tk[last, 0].T
    outs = []
    for i, (j, g) in enumerate(cols(1, last)):
        there = pl.ds(pl.multiple_of(k * FH + j, TILE), TILE)
        for mine, half in ((False, oth_d), (True, own_d)):
            sti[half, j : j + TILE] = (acci[half, j : j + TILE] + dot(tkt[half, :], g)).astype(BF)
            src, dst = sti.at[half, j : j + TILE], gin_ref.at[:, there]
            if mine:
                cp = pltpu.make_async_copy(src, dst, ls.at[2 + i])
            else:
                cp = rc(src, dst, os.at[i], orr.at[i], sib)
            cp.start()
            outs.append(cp)
    s7(last)
    for m in (4, 5, 6):
        msg(m, 25).wait_recv()
    yhs[...] = (down[last] + dr[4] + dr[5] + dr[6]).astype(BF)
    yh_msg = rc(yhs, yhr, hs.at[0], hr.at[0], yhp)
    yh_msg.start()
    for i, (j, a) in enumerate(cols(0, last)):
        there = pl.ds(pl.multiple_of(k * FH + j, TILE), TILE)
        at = a.T
        for mine, half in ((False, oth_d), (True, own_d)):
            sto[j : j + TILE, half] = (acco[j : j + TILE, half] + dot(at, tk[last, 1, :, half])).astype(BF)
            src, dst = sto.at[j : j + TILE, half], gout_ref.at[there]
            if mine:
                cp = pltpu.make_async_copy(src, dst, ls.at[5 + i])
            else:
                cp = rc(src, dst, os.at[3 + i], orr.at[3 + i], sib)
            cp.start()
            outs.append(cp)
    for m in (1, 2, 3):
        msg(m, 25).wait_recv()
    yh_msg.wait()
    gtok_ref[...] = (down[0] + dr[1] + dr[2] + dr[3] + yhr[...].astype(F32)).astype(BF)
    for cp in outs:
        cp.wait()

    def drain(n, _):
        for i in list(range(25)) + [27]:
            msg(n, i).wait_send()

        @pl.when((n >= 1) & (n < last))
        def _():
            msg(n, 25).wait_send()

        return 0

    lax.fori_loop(0, N, drain, 0)
    for m in range(1, 8):
        tok_msg(m).wait_send()
    for cp in w_out:
        cp.wait_send()


def shards(tokens, weight_in, weight_out, upstream):
    vm = lambda *shape, dtype=BF: pltpu.VMEM(shape, dtype)
    dma = lambda *shape: pltpu.SemaphoreType.DMA(shape)
    vmem, hbm = pl.BlockSpec(memory_space=pltpu.VMEM), pl.BlockSpec(memory_space=pl.ANY)
    return pl.pallas_call(
        kernel,
        out_shape=(
            jax.ShapeDtypeStruct((TB, DH), BF),
            jax.ShapeDtypeStruct((DH, 2 * FH), BF),
            jax.ShapeDtypeStruct((2 * FH, DH), BF),
        ),
        in_specs=[vmem, hbm, hbm, vmem],
        out_specs=(vmem, hbm, hbm),
        scratch_shapes=[
            vm(DC, FH), vm(FH, DC), vm(N, 2, TB, DC),
            vm(N, 2, TB, FP), vm(N, 2, 64, FP), vm(N, 2, 64, FP), vm(N, 6, 16, FP), vm(N, 2, 16, FP), vm(N, 2, TB, FP),
            vm(N, 2, TB, FQ), vm(N, 6, 32, FQ), vm(N, 2, 32, FQ), vm(N, 2, 16, FQ, dtype=F32), vm(N, 2, 16, FQ), vm(N, 2, 16, FQ), vm(N, 2, TB, FQ),
            vm(DC, FH, dtype=F32), vm(FH, DC, dtype=F32), vm(DC, FH), vm(FH, DC),
            vm(N, TB, DH, dtype=F32), vm(N, TB, DH, dtype=F32), vm(N, TB, DH, dtype=F32), vm(N, TB, DH, dtype=F32),
            vm(TB, DH), vm(TB, DH), vm(DC, TB),
            dma(N, 28), dma(N, 28), dma(8), dma(2), dma(2), dma(6), dma(6), dma(1), dma(1),
        ],
        compiler_params=pltpu.CompilerParams(
            collective_id=0, has_side_effects=True, vmem_limit_bytes=62 << 20
        ),
    )(tokens, weight_in, weight_out, upstream)


def solution(mesh):
    placed = (P("col", "row"), P("row", "col"), P("col", "row"), P("col", "row"))
    return jax.shard_map(
        shards,
        mesh=mesh,
        in_specs=placed,
        out_specs=(P("col", "row"), P("row", "col"), P("col", "row")),
        check_vma=False,
    )
```

```python
import jax
import jax.numpy as jnp
from jax import lax
from jax.experimental import pallas as pl
from jax.experimental.pallas import tpu as pltpu
from jax.sharding import PartitionSpec as P

coef = 0.7978845608
cubic = 0.044715
BF = jnp.bfloat16
F32 = jnp.float32
MESH = pl.DeviceIdType.MESH

N = 8
TB = 128
DH = 384
DC = 768
FH = 1536
FP = 640
FQ = 896
RECV = {0: 0, 1: 1, 3: 2, 2: 3, 4: 3, 5: 3, 6: 3, 7: 4, 8: 5, 9: 6, 10: 6, 11: 7}
RECV |= {13: 8, 15: 9, 14: 10, 16: 10, 17: 10, 18: 10, 12: 11, 19: 12, 20: 13, 21: 14, 22: 15, 23: 15, 24: 16}
QT = ((0, 512), (512, FQ - 512))
TILES = ((0, FP),) + tuple((FP + j, size) for j, size in QT)


def activate(hidden, back):
    inner = coef * (hidden + cubic * hidden * hidden * hidden)
    tangent = jnp.tanh(inner)
    value = 0.5 * hidden * (1.0 + tangent)
    slope = 0.5 * (1.0 + tangent) + 0.5 * hidden * (1.0 - tangent * tangent) * coef * (
        1.0 + 3.0 * cubic * hidden * hidden
    )
    return value.astype(BF), (back * slope).astype(BF)


def dot(left, right):
    return jnp.dot(left, right, preferred_element_type=F32)


def dot_nt(left, right):
    return lax.dot_general(
        left, right, (((1,), (1,)), ((), ())), preferred_element_type=F32
    )


def kernel(
    tok_ref, win_ref, wout_ref, up_ref,
    gtok_ref, gin_ref, gout_ref,
    wi, wo, tk, pp, yp, s1, rzp, szp, gp, pq, rzq, szq, kq, syq, yq, gq,
    acci, acco, sti, sto, down, doth, dsib, dr, yhs, yhr, tkt,
    ss, rs, rs25, rs26, rs27, ls, ws, wr, os, orr, hs, hr,
):
    r, c = lax.axis_index("row"), lax.axis_index("col")
    yl, z, k = r // 8, (r // 2) % 4, r % 2
    yh, x = c // 4, c % 4
    zr, zl, z2 = (z + 1) % 4, (z + 3) % 4, (z + 2) % 4

    def at_row(yl_, z_, k_):
        return (yl_ * 8 + z_ * 2 + k_, c)

    def at_col(yh_, x_):
        return (r, yh_ * 4 + x_)

    sib, ypart = at_row(yl, z, 1 - k), at_row(1 - yl, z, k)
    right, left = at_row(yl, zr, k), at_row(yl, zl, k)
    yhp = at_col(1 - yh, x)
    xr, xl, xx = at_col(yh, (x + 1) % 4), at_col(yh, (x + 3) % 4), at_col(yh, (x + 2) % 4)

    def rc(src, dst, send, recv, dev):
        return pltpu.make_async_remote_copy(
            src_ref=src, dst_ref=dst, send_sem=send, recv_sem=recv,
            device_id=dev, device_id_type=MESH,
        )

    def rows(i, size):
        return pl.ds(pl.multiple_of(i * size, size), size)

    def landed(ref, sem):
        pltpu.make_async_copy(ref, ref, sem).wait()

    def msg(n, i):
        own_p = pl.ds(pl.multiple_of(yl * 64 + z * 16, 16), 16)
        left_p = pl.ds(pl.multiple_of(yl * 64 + zl * 16, 16), 16)
        right_p = pl.ds(pl.multiple_of(yl * 64 + zr * 16, 16), 16)
        own_q = pl.ds(pl.multiple_of(z * 32 + yl * 16, 16), 16)
        if i == 0:
            src, dst, dev = pp.at[n, :, rows(1 - yl, 64)], yp.at[n], ypart
        elif i == 1:
            src, dst, dev = s1.at[n, 0, rows(z2, 16)], rzp.at[n, 0], right
        elif i == 2:
            src, dst, dev = s1.at[n, 1, rows(zr, 16)], rzp.at[n, 2], right
        elif i == 3:
            src, dst, dev = s1.at[n, 1, rows(z2, 16)], rzp.at[n, 1], left
        elif i == 4:
            src, dst, dev = s1.at[n, 0, rows(zl, 16)], rzp.at[n, 3], left
        elif i == 5:
            src, dst, dev = szp.at[n, 0], rzp.at[n, 4], right
        elif i == 6:
            src, dst, dev = szp.at[n, 1], rzp.at[n, 5], left
        elif i in (7, 8):
            src = dst = gp.at[n, :, own_p]
            dev = right if i == 7 else left
        elif i == 9:
            src = dst = gp.at[n, 0, left_p]
            dev = right
        elif i == 10:
            src = dst = gp.at[n, 1, right_p]
            dev = left
        elif i == 11:
            src = dst = gp.at[n, :, rows(yl, 64)]
            dev = ypart
        elif i == 12:
            src, dst, dev = syq.at[n], yq.at[n], ypart
        elif i == 13:
            src, dst, dev = pq.at[n, 0, rows(z2, 32)], rzq.at[n, 0], right
        elif i == 14:
            src, dst, dev = pq.at[n, 1, rows(zr, 32)], rzq.at[n, 2], right
        elif i == 15:
            src, dst, dev = pq.at[n, 1, rows(z2, 32)], rzq.at[n, 1], left
        elif i == 16:
            src, dst, dev = pq.at[n, 0, rows(zl, 32)], rzq.at[n, 3], left
        elif i == 17:
            src, dst, dev = szq.at[n, 0], rzq.at[n, 4], right
        elif i == 18:
            src, dst, dev = szq.at[n, 1], rzq.at[n, 5], left
        elif i == 19:
            src = dst = gq.at[n, :, own_q]
            dev = ypart
        elif i in (20, 21):
            src = dst = gq.at[n, :, rows(z, 32)]
            dev = right if i == 20 else left
        elif i == 22:
            src = dst = gq.at[n, 0, rows(zl, 32)]
            dev = right
        elif i == 23:
            src = dst = gq.at[n, 1, rows(zr, 32)]
            dev = left
        elif i == 24:
            src, dst, dev = doth.at[n], dsib.at[n], sib
        elif i == 25:
            m, later = (n - 1) % 3, (n - 1) // 3
            dx = (1 - later) * (1 + 2 * m - 3 * (m // 2)) + later * (2 - m + 3 * (m // 2))
            src, dst, dev = down.at[n], dr.at[n], at_col(yh, (x + dx) % 4)
        elif i == 27:
            src = dst = tk.at[n, :, :, own_d]
            dev = sib
        if i == 27:
            recv = rs27.at[n]
        elif i == 25:
            recv = rs25.at[(n - 1) // 3]
        else:
            recv = rs.at[n % 4, RECV[i]]
        return rc(src, dst, ss.at[N if i == 25 else n], recv, dev)

    own_d = pl.ds(pl.multiple_of(k * DH, DH), DH)
    oth_d = pl.ds(pl.multiple_of((1 - k) * DH, DH), DH)
    own_f = pl.ds(pl.multiple_of(k * FH, FH), FH)
    oth_f = pl.ds(pl.multiple_of((1 - k) * FH, FH), FH)

    def tok_msg(m):
        dev = {1: xl, 2: xr, 3: xx, 4: xx, 5: xl, 6: xr, 7: yhp}[m]
        src = tk.at[0 if m in (1, 2, 3, 7) else 7, :, :, own_d]
        return rc(src, tk.at[m, :, :, own_d], ss.at[N + 1], rs26.at[m], dev)

    w_own, w_out = [], []
    for i, (j, size) in enumerate(TILES):
        mine = pl.ds(pl.multiple_of(k * FH + j, 128), size)
        other = pl.ds(pl.multiple_of((1 - k) * FH + j, 128), size)
        here = pl.ds(j, size)
        w_own += [
            pltpu.make_async_copy(win_ref.at[:, mine], wi.at[own_d, here], ls.at[2 * i]),
            pltpu.make_async_copy(wout_ref.at[mine], wo.at[here, own_d], ls.at[2 * i + 1]),
        ]
        w_out += [
            rc(win_ref.at[:, other], wi.at[own_d, here], ws.at[2 * i], wr.at[2 * i], sib),
            rc(wout_ref.at[other], wo.at[here, own_d], ws.at[2 * i + 1], wr.at[2 * i + 1], sib),
        ]
    w_order = [2, 3, 4, 5, 0, 1]
    for i in w_order:
        w_own[i].start()
    tk[0, 0, :, own_d] = tok_ref[...]
    tk[0, 1, :, own_d] = up_ref[...]

    barrier = pltpu.get_barrier_semaphore()
    partners = (sib, ypart, right, left, yhp, xr, xl, xx)
    for dev in partners:
        pl.semaphore_signal(barrier, inc=1, device_id=dev, device_id_type=MESH)
    pl.semaphore_wait(barrier, len(partners))

    msg(0, 27).start()
    tok_msg(7).start()
    for i in w_order:
        w_out[i].start()
    for m in (1, 2, 3):
        tok_msg(m).start()

    def weights(n, tile):
        @pl.when(n == 0)
        def _():
            for i in (2 * tile, 2 * tile + 1):
                w_own[i].wait()
                w_out[i].wait_recv()

    def zero(n):
        @pl.when(n == 2)
        def _():
            acci[...] = jnp.zeros_like(acci)
            acco[...] = jnp.zeros_like(acco)

    def total(*refs):
        out = refs[0].astype(F32)
        for ref in refs[1:]:
            out = out + ref.astype(F32)
        return out

    def start(n, *copies):
        for i in copies:
            msg(n, i).start()

    def arrived(n, *copies):
        for i in copies:
            msg(n, i).wait_recv()

    def p0(n):
        weights(n, 0)
        pp[n, 0] = dot(tk[n, 0], wi[:, 0:FP]).astype(BF)
        pp[n, 1] = dot_nt(tk[n, 1], wo[0:FP, :]).astype(BF)
        start(n, 0)

    def q0(n):
        arrived(n, 27)
        for i, (j, size) in enumerate(QT):
            weights(n, 1 + i)
            pq[n, 0, :, j : j + size] = dot(tk[n, 0], wi[:, FP + j : FP + j + size]).astype(BF)
            pq[n, 1, :, j : j + size] = dot_nt(tk[n, 1], wo[FP + j : FP + j + size, :]).astype(BF)
        start(n, 13, 15, 14, 16)

    def p1(n):
        arrived(n, 0)
        s1[n] = total(pp[n, :, rows(yl, 64)], yp[n]).astype(BF)
        start(n, 1, 3, 2, 4)

    def q1a(n):
        arrived(n, 13)
        szq[n, 0] = total(pq[n, 0, rows(zr, 32)], rzq[n, 0]).astype(BF)
        start(n, 17)

    def q1b(n):
        arrived(n, 15)
        szq[n, 1] = total(pq[n, 1, rows(zl, 32)], rzq[n, 1]).astype(BF)
        start(n, 18)

    def p2a(n):
        arrived(n, 1)
        szp[n, 0] = total(s1[n, 0, rows(zr, 16)], rzp[n, 0]).astype(BF)
        start(n, 5)

    def p2b(n):
        arrived(n, 3)
        szp[n, 1] = total(s1[n, 1, rows(zl, 16)], rzp[n, 1]).astype(BF)
        start(n, 6)

    def q2(n):
        landed(rzq.at[n, pl.ds(2, 4)], rs.at[n % 4, RECV[14]])
        for t, a, b in ((0, 3, 4), (1, 2, 5)):
            for mine in (False, True):
                half = yl if mine else 1 - yl
                here = pl.ds(pl.multiple_of(z * 32 + half * 16, 16), 16)
                sums = total(pq[n, t, here], rzq[n, a, rows(half, 16)], rzq[n, b, rows(half, 16)])
                if mine:
                    kq[n, t] = sums
                else:
                    syq[n, t] = sums.astype(BF)
        start(n, 12)

    def p3(n):
        landed(rzp.at[n, pl.ds(2, 4)], rs.at[n % 4, RECV[2]])
        hidden = total(s1[n, 0, rows(z, 16)], rzp[n, 3], rzp[n, 4])
        back = total(s1[n, 1, rows(z, 16)], rzp[n, 2], rzp[n, 5])
        here = pl.ds(pl.multiple_of(yl * 64 + z * 16, 16), 16)
        gp[n, 0, here], gp[n, 1, here] = activate(hidden, back)
        start(n, 7, 8)

    def q3(n):
        arrived(n, 12)
        here = pl.ds(pl.multiple_of(z * 32 + yl * 16, 16), 16)
        gq[n, 0, here], gq[n, 1, here] = activate(total(kq[n, 0], yq[n, 0]), total(kq[n, 1], yq[n, 1]))
        start(n, 19)

    def p4a(n):
        arrived(n, 7)
        start(n, 9)

    def p4b(n):
        arrived(n, 8)
        start(n, 10)

    def q4(n):
        arrived(n, 19)
        start(n, 20, 21)

    def p5(n):
        landed(gp.at[n, :, pl.ds(pl.multiple_of(yl * 64 + z2 * 16, 16), 16)], rs.at[n % 4, RECV[9]])
        start(n, 11)

    def q5a(n):
        arrived(n, 20)
        start(n, 22)

    def q5b(n):
        arrived(n, 21)
        start(n, 23)

    def s6_wait(n):
        landed(gq.at[n, :, rows(z2, 32)], rs.at[n % 4, RECV[22]])
        arrived(n, 11)

    def cols(t, n):
        yield 0, FP, gp[n, t]
        for j, size in QT:
            yield FP + j, size, gq[n, t, :, j : j + size]

    def grads(n):
        s6_wait(n)
        for half, ref in ((oth_d, doth), (own_d, down)):
            ref[n] = dot_nt(gp[n, 1], wi[half, 0:FP]) + dot_nt(gq[n, 1], wi[half, FP:FH])
            if ref is doth:
                start(n, 24)
        tkt[...] = tk[n, 0].T
        for j, size, g in cols(1, n):
            acci[:, j : j + size] += dot(tkt[...], g)
        for j, size, a in cols(0, n):
            acco[j : j + size, :] += dot(a.T, tk[n, 1])

    def s7(n):
        arrived(n, 24)
        down[n] += dsib[n]

    def width_sums(n):
        s7(n)

        @pl.when(n >= 1)
        def _():
            start(n, 25)

    def tokens_in(n):
        @pl.when(n == 0)
        def _():
            tok_msg(7).wait_recv()
            for m in (4, 5, 6):
                tok_msg(m).start()
            start(7, 27)

        for m in range(1, 7):

            @pl.when(n == m - 1)
            def _():
                tok_msg(m).wait_recv()
                start(m, 27)

    order = (
        (p5, 5), (q0, 0), (q1a, 1), (p3, 3), (p4a, 4), (p4b, 4), (p2b, 2), (q1b, 1), (p2a, 2), (p0, 0), (q2, 2), (p1, 1),
        (q4, 4), (q5a, 5), (q5b, 5), (q3, 3), (tokens_in, 0), (zero, 0), (width_sums, 7), (grads, 6),
    )

    def step(n, _):
        for op, late in order:

            @pl.when((n >= late) & (n < N + late))
            def _():
                op(n - late)

        return 0

    lax.fori_loop(0, N + 5, step, 0)

    last = N - 1
    s7(last - 1)
    start(last - 1, 25)
    s6_wait(last)
    for half, ref in ((oth_d, doth), (own_d, down)):
        ref[last] = dot_nt(gp[last, 1], wi[half, 0:FP]) + dot_nt(gq[last, 1], wi[half, FP:FH])
        if ref is doth:
            msg(last, 24).start()
    tkt[...] = tk[last, 0].T
    outs = []
    for i, (j, size, g) in enumerate(cols(1, last)):
        there = pl.ds(pl.multiple_of(k * FH + j, 128), size)
        for mine, half in ((False, oth_d), (True, own_d)):
            sti[half, j : j + size] = (acci[half, j : j + size] + dot(tkt[half, :], g)).astype(BF)
            src, dst = sti.at[half, j : j + size], gin_ref.at[:, there]
            if mine:
                cp = pltpu.make_async_copy(src, dst, ls.at[6 + i])
            else:
                cp = rc(src, dst, os.at[i], orr.at[i], sib)
            cp.start()
            outs.append(cp)
    s7(last)
    landed(dr.at[pl.ds(4, 3)], rs25.at[1])
    yhs[...] = (down[last] + dr[4] + dr[5] + dr[6]).astype(BF)
    yh_msg = rc(yhs, yhr, hs.at[0], hr.at[0], yhp)
    yh_msg.start()
    for i, (j, size, a) in enumerate(cols(0, last)):
        there = pl.ds(pl.multiple_of(k * FH + j, 128), size)
        at = a.T
        for mine, half in ((False, oth_d), (True, own_d)):
            sto[j : j + size, half] = (acco[j : j + size, half] + dot(at, tk[last, 1, :, half])).astype(BF)
            src, dst = sto.at[j : j + size, half], gout_ref.at[there]
            if mine:
                cp = pltpu.make_async_copy(src, dst, ls.at[9 + i])
            else:
                cp = rc(src, dst, os.at[3 + i], orr.at[3 + i], sib)
            cp.start()
            outs.append(cp)
    landed(dr.at[pl.ds(1, 3)], rs25.at[0])
    yh_msg.wait()
    gtok_ref[...] = (down[0] + dr[1] + dr[2] + dr[3] + yhr[...].astype(F32)).astype(BF)
    for cp in outs:
        cp.wait()

    for n in range(N):
        landed(wo.at[pl.ds(0, 1152)], ss.at[n])
    landed(wo.at[pl.ds(0, 768)], ss.at[N])
    landed(wo.at[pl.ds(0, 896)], ss.at[N + 1])
    for cp in w_out:
        cp.wait_send()


def shards(tokens, weight_in, weight_out, upstream):
    vm = lambda *shape, dtype=BF: pltpu.VMEM(shape, dtype)
    dma = lambda *shape: pltpu.SemaphoreType.DMA(shape)
    vmem, hbm = pl.BlockSpec(memory_space=pltpu.VMEM), pl.BlockSpec(memory_space=pl.ANY)
    return pl.pallas_call(
        kernel,
        out_shape=(
            jax.ShapeDtypeStruct((TB, DH), BF),
            jax.ShapeDtypeStruct((DH, 2 * FH), BF),
            jax.ShapeDtypeStruct((2 * FH, DH), BF),
        ),
        in_specs=[vmem, hbm, hbm, vmem],
        out_specs=(vmem, hbm, hbm),
        scratch_shapes=[
            vm(DC, FH), vm(FH, DC), vm(N, 2, TB, DC),
            vm(N, 2, TB, FP), vm(N, 2, 64, FP), vm(N, 2, 64, FP), vm(N, 6, 16, FP), vm(N, 2, 16, FP), vm(N, 2, TB, FP),
            vm(N, 2, TB, FQ), vm(N, 6, 32, FQ), vm(N, 2, 32, FQ), vm(N, 2, 16, FQ, dtype=F32), vm(N, 2, 16, FQ), vm(N, 2, 16, FQ), vm(N, 2, TB, FQ),
            vm(DC, FH, dtype=F32), vm(FH, DC, dtype=F32), vm(DC, FH), vm(FH, DC),
            vm(N, TB, DH, dtype=F32), vm(N, TB, DH, dtype=F32), vm(N, TB, DH, dtype=F32), vm(N, TB, DH, dtype=F32),
            vm(TB, DH), vm(TB, DH), vm(DC, TB),
            dma(N + 2), dma(4, 17), dma(2), dma(N), dma(N), dma(12), dma(6), dma(6), dma(6), dma(6), dma(1), dma(1),
        ],
        compiler_params=pltpu.CompilerParams(
            collective_id=0, has_side_effects=True, vmem_limit_bytes=62 << 20
        ),
    )(tokens, weight_in, weight_out, upstream)


def solution(mesh):
    placed = (P("col", "row"), P("row", "col"), P("col", "row"), P("col", "row"))
    return jax.shard_map(
        shards,
        mesh=mesh,
        in_specs=placed,
        out_specs=(P("col", "row"), P("row", "col"), P("col", "row")),
        check_vma=False,
    )
```

```python
import jax
import jax.numpy as jnp
from jax import lax
from jax.experimental import pallas as pl
from jax.experimental.pallas import tpu as pltpu
from jax.sharding import PartitionSpec as P

coef = 0.7978845608
cubic = 0.044715
BF = jnp.bfloat16
F32 = jnp.float32
MESH = pl.DeviceIdType.MESH

N = 8
TB = 128
DH = 384
DC = 768
FH = 1536
FP = 640
FQ = 896
RECV = {0: 0, 1: 1, 3: 2, 2: 3, 4: 3, 5: 3, 6: 3, 7: 4, 8: 5, 9: 6, 10: 6, 11: 7}
RECV |= {13: 8, 15: 9, 14: 10, 16: 10, 17: 10, 18: 10, 12: 11, 19: 12, 20: 13, 21: 14, 22: 15, 23: 15, 24: 16, 28: 17}
QT = ((0, 512), (512, FQ - 512))
TILES = ((0, FP),) + tuple((FP + j, size) for j, size in QT)


def activate(hidden, back):
    inner = coef * (hidden + cubic * hidden * hidden * hidden)
    tangent = jnp.tanh(inner)
    value = 0.5 * hidden * (1.0 + tangent)
    slope = 0.5 * (1.0 + tangent) + 0.5 * hidden * (1.0 - tangent * tangent) * coef * (
        1.0 + 3.0 * cubic * hidden * hidden
    )
    return value.astype(BF), (back * slope).astype(BF)


def dot(left, right):
    return jnp.dot(left, right, preferred_element_type=F32)


def dot_nt(left, right):
    return lax.dot_general(
        left, right, (((1,), (1,)), ((), ())), preferred_element_type=F32
    )


def kernel(
    tok_ref, win_ref, wout_ref, up_ref,
    gtok_ref, gin_ref, gout_ref,
    wi, wo, tk, ppf, ppo, pp, yp, s1, rzp, szp, gp, pq, rzq, szq, kq, syq, yq, gq,
    acci, acco, sti, sto, down, doth, dsib, dr, yhs, yhr, tkt,
    ss, rs, rs25, rs26, rs27, ls, ws, wr, os, orr, hs, hr,
):
    r, c = lax.axis_index("row"), lax.axis_index("col")
    yl, z, k = r // 8, (r // 2) % 4, r % 2
    yh, x = c // 4, c % 4
    zr, zl, z2 = (z + 1) % 4, (z + 3) % 4, (z + 2) % 4

    def at_row(yl_, z_, k_):
        return (yl_ * 8 + z_ * 2 + k_, c)

    def at_col(yh_, x_):
        return (r, yh_ * 4 + x_)

    sib, ypart = at_row(yl, z, 1 - k), at_row(1 - yl, z, k)
    right, left = at_row(yl, zr, k), at_row(yl, zl, k)
    yhp = at_col(1 - yh, x)
    xr, xl, xx = at_col(yh, (x + 1) % 4), at_col(yh, (x + 3) % 4), at_col(yh, (x + 2) % 4)

    def rc(src, dst, send, recv, dev):
        return pltpu.make_async_remote_copy(
            src_ref=src, dst_ref=dst, send_sem=send, recv_sem=recv,
            device_id=dev, device_id_type=MESH,
        )

    def rows(i, size):
        return pl.ds(pl.multiple_of(i * size, size), size)

    def landed(ref, sem):
        pltpu.make_async_copy(ref, ref, sem).wait()

    def msg(n, i):
        own_p = pl.ds(pl.multiple_of(yl * 64 + z * 16, 16), 16)
        left_p = pl.ds(pl.multiple_of(yl * 64 + zl * 16, 16), 16)
        right_p = pl.ds(pl.multiple_of(yl * 64 + zr * 16, 16), 16)
        own_q = pl.ds(pl.multiple_of(z * 32 + yl * 16, 16), 16)
        if i == 0:
            src, dst, dev = pp.at[n], yp.at[n], ypart
        elif i == 1:
            src, dst, dev = s1.at[n, 0, rows(z2, 16)], rzp.at[n, 0], right
        elif i == 2:
            src, dst, dev = s1.at[n, 1, rows(zr, 16)], rzp.at[n, 2], right
        elif i == 3:
            src, dst, dev = s1.at[n, 1, rows(z2, 16)], rzp.at[n, 1], left
        elif i == 4:
            src, dst, dev = s1.at[n, 0, rows(zl, 16)], rzp.at[n, 3], left
        elif i == 5:
            src, dst, dev = szp.at[n, 0], rzp.at[n, 4], right
        elif i == 6:
            src, dst, dev = szp.at[n, 1], rzp.at[n, 5], left
        elif i in (7, 8):
            src = dst = gp.at[n, :, own_p]
            dev = right if i == 7 else left
        elif i == 9:
            src = dst = gp.at[n, 0, left_p]
            dev = right
        elif i == 10:
            src = dst = gp.at[n, 1, right_p]
            dev = left
        elif i == 11:
            src = dst = gp.at[n, 1, rows(yl, 64)]
            dev = ypart
        elif i == 28:
            src = dst = gp.at[n, 0, rows(yl, 64)]
            dev = ypart
        elif i == 12:
            src, dst, dev = syq.at[n], yq.at[n], ypart
        elif i == 13:
            src, dst, dev = pq.at[n, 0, rows(z2, 32)], rzq.at[n, 0], right
        elif i == 14:
            src, dst, dev = pq.at[n, 1, rows(zr, 32)], rzq.at[n, 2], right
        elif i == 15:
            src, dst, dev = pq.at[n, 1, rows(z2, 32)], rzq.at[n, 1], left
        elif i == 16:
            src, dst, dev = pq.at[n, 0, rows(zl, 32)], rzq.at[n, 3], left
        elif i == 17:
            src, dst, dev = szq.at[n, 0], rzq.at[n, 4], right
        elif i == 18:
            src, dst, dev = szq.at[n, 1], rzq.at[n, 5], left
        elif i == 19:
            src = dst = gq.at[n, :, own_q]
            dev = ypart
        elif i in (20, 21):
            src = dst = gq.at[n, :, rows(z, 32)]
            dev = right if i == 20 else left
        elif i == 22:
            src = dst = gq.at[n, 0, rows(zl, 32)]
            dev = right
        elif i == 23:
            src = dst = gq.at[n, 1, rows(zr, 32)]
            dev = left
        elif i == 24:
            src, dst, dev = doth.at[n], dsib.at[n], sib
        elif i == 25:
            m, later = (n - 1) % 3, (n - 1) // 3
            dx = (1 - later) * (1 + 2 * m - 3 * (m // 2)) + later * (2 - m + 3 * (m // 2))
            src, dst, dev = down.at[n], dr.at[n], at_col(yh, (x + dx) % 4)
        elif i == 27:
            src = dst = tk.at[n, :, :, own_d]
            dev = sib
        if i == 27:
            recv = rs27.at[n]
        elif i == 25:
            recv = rs25.at[(n - 1) // 3]
        else:
            recv = rs.at[n, RECV[i]]
        return rc(src, dst, ss.at[N if i == 25 else n], recv, dev)

    own_d = pl.ds(pl.multiple_of(k * DH, DH), DH)
    oth_d = pl.ds(pl.multiple_of((1 - k) * DH, DH), DH)
    own_f = pl.ds(pl.multiple_of(k * FH, FH), FH)
    oth_f = pl.ds(pl.multiple_of((1 - k) * FH, FH), FH)

    def tok_msg(m):
        dev = {1: xl, 2: xr, 3: xx, 4: xx, 5: xl, 6: xr, 7: yhp}[m]
        src = tk.at[0 if m in (1, 2, 3, 7) else 7, :, :, own_d]
        return rc(src, tk.at[m, :, :, own_d], ss.at[N + 1], rs26.at[m], dev)

    barrier = pltpu.get_barrier_semaphore()
    partners = (sib, ypart, right, left, yhp, xr, xl, xx)
    for dev in partners:
        pl.semaphore_signal(barrier, inc=1, device_id=dev, device_id_type=MESH)

    w_own, w_out = [], []
    for i, (j, size) in enumerate(TILES):
        mine = pl.ds(pl.multiple_of(k * FH + j, 128), size)
        other = pl.ds(pl.multiple_of((1 - k) * FH + j, 128), size)
        here = pl.ds(j, size)
        w_own += [
            pltpu.make_async_copy(win_ref.at[:, mine], wi.at[own_d, here], ls.at[2 * i]),
            pltpu.make_async_copy(wout_ref.at[mine], wo.at[here, own_d], ls.at[2 * i + 1]),
        ]
        w_out += [
            rc(win_ref.at[:, other], wi.at[own_d, here], ws.at[2 * i], wr.at[2 * i], sib),
            rc(wout_ref.at[other], wo.at[here, own_d], ws.at[2 * i + 1], wr.at[2 * i + 1], sib),
        ]
    w_order = range(6)
    for i in w_order:
        w_own[i].start()
    t_own = [
        pltpu.make_async_copy(ref, tk.at[0, i, :, own_d], ls.at[12 + i])
        for i, ref in enumerate((tok_ref, up_ref))
    ]
    for cp in t_own:
        cp.start()
    pl.semaphore_wait(barrier, len(partners))
    for cp in t_own:
        cp.wait()

    msg(0, 27).start()
    tok_msg(7).start()
    for i in w_order:
        w_out[i].start()
    tok_msg(1).start()
    tok_msg(2).start()

    def weights(n, tile):
        @pl.when(n == 0)
        def _():
            for i in (2 * tile, 2 * tile + 1):
                w_own[i].wait()
                w_out[i].wait_recv()

    def zero(n):
        @pl.when(n == 2)
        def _():
            acci[...] = jnp.zeros_like(acci)
            acco[...] = jnp.zeros_like(acco)

    def total(*refs):
        out = refs[0].astype(F32)
        for ref in refs[1:]:
            out = out + ref.astype(F32)
        return out

    def start(n, *copies):
        for i in copies:
            msg(n, i).start()

    def arrived(n, *copies):
        for i in copies:
            msg(n, i).wait_recv()

    def p0(n):
        arrived(n, 27)
        weights(n, 0)
        ppf[0] = dot(tk[n, 0], wi[:, 0:FP])
        ppf[1] = dot_nt(tk[n, 1], wo[0:FP, :])
        pp[n] = ppf[:, rows(1 - yl, 64)].astype(BF)
        start(n, 0)
        ppo[n] = ppf[:, rows(yl, 64)]

    def q0(n):
        for i, (j, size) in enumerate(QT):
            weights(n, 1 + i)
            pq[n, 0, :, j : j + size] = dot(tk[n, 0], wi[:, FP + j : FP + j + size]).astype(BF)
            pq[n, 1, :, j : j + size] = dot_nt(tk[n, 1], wo[FP + j : FP + j + size, :]).astype(BF)
        start(n, 13, 15, 14, 16)

    def p1(n):
        arrived(n, 0)
        s1[n] = total(ppo[n], yp[n]).astype(BF)
        start(n, 1, 3, 2, 4)

    def q1a(n):
        arrived(n, 13)
        szq[n, 0] = total(pq[n, 0, rows(zr, 32)], rzq[n, 0]).astype(BF)
        start(n, 17)

    def q1b(n):
        arrived(n, 15)
        szq[n, 1] = total(pq[n, 1, rows(zl, 32)], rzq[n, 1]).astype(BF)
        start(n, 18)

    def p2a(n):
        arrived(n, 1)
        szp[n, 0] = total(ppo[n, 0, rows(zr, 16)], yp[n, 0, rows(zr, 16)], rzp[n, 0]).astype(BF)
        start(n, 5)

    def p2b(n):
        arrived(n, 3)
        szp[n, 1] = total(ppo[n, 1, rows(zl, 16)], yp[n, 1, rows(zl, 16)], rzp[n, 1]).astype(BF)
        start(n, 6)

    def q2(n):
        landed(rzq.at[n, pl.ds(2, 4)], rs.at[n, RECV[14]])
        for t, a, b in ((0, 3, 4), (1, 2, 5)):
            for mine in (False, True):
                half = yl if mine else 1 - yl
                here = pl.ds(pl.multiple_of(z * 32 + half * 16, 16), 16)
                sums = total(pq[n, t, here], rzq[n, a, rows(half, 16)], rzq[n, b, rows(half, 16)])
                if mine:
                    kq[n, t] = sums
                else:
                    syq[n, t] = sums.astype(BF)
        start(n, 12)

    def p3(n):
        landed(rzp.at[n, pl.ds(2, 4)], rs.at[n, RECV[2]])
        hidden = total(ppo[n, 0, rows(z, 16)], yp[n, 0, rows(z, 16)], rzp[n, 3], rzp[n, 4])
        back = total(ppo[n, 1, rows(z, 16)], yp[n, 1, rows(z, 16)], rzp[n, 2], rzp[n, 5])
        here = pl.ds(pl.multiple_of(yl * 64 + z * 16, 16), 16)
        gp[n, 0, here], gp[n, 1, here] = activate(hidden, back)
        start(n, 7, 8)

    def q3(n):
        arrived(n, 12)
        here = pl.ds(pl.multiple_of(z * 32 + yl * 16, 16), 16)
        gq[n, 0, here], gq[n, 1, here] = activate(total(kq[n, 0], yq[n, 0]), total(kq[n, 1], yq[n, 1]))
        start(n, 19)

    def p4a(n):
        arrived(n, 7)
        start(n, 9)

    def p4b(n):
        arrived(n, 8)
        start(n, 10)

    def q4(n):
        arrived(n, 19)
        start(n, 20, 21)

    def p5(n):
        landed(gp.at[n, :, pl.ds(pl.multiple_of(yl * 64 + z2 * 16, 16), 16)], rs.at[n, RECV[9]])
        start(n, 11, 28)

    def q5a(n):
        arrived(n, 20)
        start(n, 22)

    def q5b(n):
        arrived(n, 21)
        start(n, 23)

    def cols(t, n):
        yield 0, FP, gp[n, t]
        for j, size in QT:
            yield FP + j, size, gq[n, t, :, j : j + size]

    def grads(n):
        landed(gq.at[n, :, rows(z2, 32)], rs.at[n, RECV[22]])
        arrived(n, 11, 28)
        for half, ref in ((oth_d, doth), (own_d, down)):
            ref[n] = dot_nt(gp[n, 1], wi[half, 0:FP]) + dot_nt(gq[n, 1], wi[half, FP:FH])
            if ref is doth:
                start(n, 24)
        tkt[...] = tk[n, 0].T
        for j, size, g in cols(1, n):
            acci[:, j : j + size] += dot(tkt[...], g)
        for j, size, a in cols(0, n):
            acco[j : j + size, :] += dot(a.T, tk[n, 1])

    def s7(n):
        arrived(n, 24)
        down[n] += dsib[n]

    def width_sums(n):
        s7(n)

        @pl.when(n >= 1)
        def _():
            start(n, 25)

    def tokens_in(n):
        @pl.when(n == 0)
        def _():
            tok_msg(3).start()
            tok_msg(7).wait_recv()
            for m in (4, 5, 6):
                tok_msg(m).start()
            start(7, 27)

        for m in range(1, 7):

            @pl.when(n == m - 1)
            def _():
                tok_msg(m).wait_recv()
                start(m, 27)

    order = (
        (p0, 0), (q0, 0), (q1b, 1), (q2, 3), (p1, 2), (p4a, 5), (p3, 4), (p4b, 5), (p2b, 3),
        (q1a, 1), (q3, 4), (tokens_in, 0), (p2a, 3), (p5, 6), (q4, 5), (zero, 0), (width_sums, 9), (grads, 8), (q5a, 6), (q5b, 6),
    )

    def step(n, _):
        for op, late in order:

            @pl.when((n >= late) & (n < N + late))
            def _():
                op(n - late)

        return 0

    lax.fori_loop(0, N + 7, step, 0)

    last = N - 1
    outs = []

    def give(src, dst, i):
        outs.append(rc(src, dst, os.at[i], orr.at[i], sib))
        outs[-1].start()

    def in_tile(i):
        j, size = TILES[i]
        g = gp[last, 1] if i == 0 else gq[last, 1, :, j - FP : j - FP + size]
        there = pl.ds(pl.multiple_of(k * FH + j, 128), size)
        sti[:, j : j + size] = (acci[oth_d, j : j + size] + dot(tkt[oth_d, :], g)).astype(BF)
        give(sti.at[:, j : j + size], gin_ref.at[:, there], i)
        gin_ref[:, there] = (acci[own_d, j : j + size] + dot(tkt[own_d, :], g)).astype(BF)

    def out_tile(i):
        j, size = TILES[i]
        a = gp[last, 0] if i == 0 else gq[last, 0, :, j - FP : j - FP + size]
        there = pl.ds(pl.multiple_of(k * FH + j, 128), size)
        at = a.T
        sto[j : j + size] = (acco[j : j + size, oth_d] + dot(at, tk[last, 1, :, oth_d])).astype(BF)
        give(sto.at[j : j + size], gout_ref.at[there], 3 + i)
        gout_ref[there] = (acco[j : j + size, own_d] + dot(at, tk[last, 1, :, own_d])).astype(BF)

    s7(last - 1)
    start(last - 1, 25)
    tkt[...] = tk[last, 0].T
    landed(gq.at[last, :, rows(z2, 32)], rs.at[last, RECV[22]])
    for half, ref in ((oth_d, doth), (own_d, down)):
        ref[last] = dot_nt(gq[last, 1], wi[half, FP:FH])
    for i in (1, 2):
        in_tile(i)
        out_tile(i)
    arrived(last, 11)
    for half, ref in ((oth_d, doth), (own_d, down)):
        ref[last] += dot_nt(gp[last, 1], wi[half, 0:FP])
        if ref is doth:
            start(last, 24)
    in_tile(0)
    s7(last)
    landed(dr.at[pl.ds(4, 3)], rs25.at[1])
    yhs[...] = (down[last] + dr[4] + dr[5] + dr[6]).astype(BF)
    yh_msg = rc(yhs, yhr, hs.at[0], hr.at[0], yhp)
    yh_msg.start()
    arrived(last, 28)
    out_tile(0)
    landed(dr.at[pl.ds(1, 3)], rs25.at[0])
    yh_msg.wait()
    gtok_ref[...] = (down[0] + dr[1] + dr[2] + dr[3] + yhr[...].astype(F32)).astype(BF)
    for cp in outs:
        cp.wait()

    for n in range(N):
        landed(wo.at[pl.ds(0, 1152)], ss.at[n])
    landed(wo.at[pl.ds(0, 768)], ss.at[N])
    landed(wo.at[pl.ds(0, 896)], ss.at[N + 1])
    for cp in w_out:
        cp.wait_send()


def hand_on(gtok, gin, gout, gtok_out, gin_out, gout_out, sem):
    copies = [
        pltpu.make_async_copy(a, b, sem.at[i])
        for i, (a, b) in enumerate(((gin, gin_out), (gout, gout_out), (gtok, gtok_out)))
    ]
    for cp in copies:
        cp.start()
    for cp in copies:
        cp.wait()


def shards(tokens, weight_in, weight_out, upstream):
    vm = lambda *shape, dtype=BF: pltpu.VMEM(shape, dtype)
    dma = lambda *shape: pltpu.SemaphoreType.DMA(shape)
    vmem, hbm = pl.BlockSpec(memory_space=pltpu.VMEM), pl.BlockSpec(memory_space=pl.ANY)
    results = pl.pallas_call(
        kernel,
        out_shape=(
            vm(TB, DH),
            vm(DH, 2 * FH),
            vm(2 * FH, DH),
        ),
        in_specs=[hbm] * 4,
        out_specs=(vmem, vmem, vmem),
        scratch_shapes=[
            vm(DC, FH), vm(FH, DC), vm(N, 2, TB, DC),
            vm(2, TB, FP, dtype=F32), vm(N, 2, 64, FP, dtype=F32), vm(N, 2, 64, FP), vm(N, 2, 64, FP), vm(N, 2, 64, FP), vm(N, 6, 16, FP), vm(N, 2, 16, FP), vm(N, 2, TB, FP),
            vm(N, 2, TB, FQ), vm(N, 6, 32, FQ), vm(N, 2, 32, FQ), vm(N, 2, 16, FQ, dtype=F32), vm(N, 2, 16, FQ), vm(N, 2, 16, FQ), vm(N, 2, TB, FQ),
            vm(DC, FH, dtype=F32), vm(FH, DC, dtype=F32), vm(DH, FH), vm(FH, DH),
            vm(N, TB, DH, dtype=F32), vm(N, TB, DH, dtype=F32), vm(N, TB, DH, dtype=F32), vm(N, TB, DH, dtype=F32),
            vm(TB, DH), vm(TB, DH), vm(DC, TB),
            dma(N + 2), dma(N, 18), dma(2), dma(N), dma(N), dma(14), dma(6), dma(6), dma(6), dma(6), dma(1), dma(1),
        ],
        compiler_params=pltpu.CompilerParams(
            collective_id=0, has_side_effects=True, vmem_limit_bytes=53 << 20
        ),
    )(tokens, weight_in, weight_out, upstream)
    return pl.pallas_call(
        hand_on,
        out_shape=tuple(jax.ShapeDtypeStruct(a.shape, a.dtype) for a in results),
        in_specs=[vmem] * 3,
        out_specs=(hbm,) * 3,
        scratch_shapes=[dma(3)],
        compiler_params=pltpu.CompilerParams(vmem_limit_bytes=1 << 20),
    )(*(pltpu.with_memory_space_constraint(a, pltpu.VMEM) for a in results))


def solution(mesh):
    placed = (P("col", "row"), P("row", "col"), P("col", "row"), P("col", "row"))
    return jax.shard_map(
        shards,
        mesh=mesh,
        in_specs=placed,
        out_specs=(P("col", "row"), P("row", "col"), P("col", "row")),
        check_vma=False,
    )
```

```python
import jax
import jax.numpy as jnp
from jax import lax
from jax.experimental import pallas as pl
from jax.experimental.pallas import tpu as pltpu
from jax.sharding import PartitionSpec as P

coef = 0.7978845608
cubic = 0.044715
BF = jnp.bfloat16
F32 = jnp.float32
MESH = pl.DeviceIdType.MESH

N = 8
TB = 128
DH = 384
DC = 768
FH = 1536
FP = 640
FQ = 896
RECV = {0: 0, 1: 1, 3: 2, 2: 3, 4: 3, 5: 3, 6: 3, 7: 4, 8: 5, 9: 6, 10: 6, 11: 7}
RECV |= {13: 8, 15: 9, 14: 10, 16: 10, 17: 10, 18: 10, 12: 11, 19: 12, 20: 13, 21: 14, 22: 15, 23: 15, 24: 16, 28: 17}
QT = ((0, 512), (512, FQ - 512))
TILES = ((0, FP),) + tuple((FP + j, size) for j, size in QT)


def activate(hidden, back):
    inner = coef * (hidden + cubic * hidden * hidden * hidden)
    tangent = jnp.tanh(inner)
    value = 0.5 * hidden * (1.0 + tangent)
    slope = 0.5 * (1.0 + tangent) + 0.5 * hidden * (1.0 - tangent * tangent) * coef * (
        1.0 + 3.0 * cubic * hidden * hidden
    )
    return value.astype(BF), (back * slope).astype(BF)


def dot(left, right):
    return jnp.dot(left, right, preferred_element_type=F32)


def dot_nt(left, right):
    return lax.dot_general(
        left, right, (((1,), (1,)), ((), ())), preferred_element_type=F32
    )


def kernel(
    tok_ref, win_ref, wout_ref, up_ref,
    gtok_ref, gin_ref, gout_ref,
    wi, wo, tk, ppf, ppo, pp, yp, s1, rzp, szp, gp, pq, rzq, szq, kq, syq, yq, gq,
    acci, acco, sti, sto, down, doth, dsib, dr, yhs, yhr, tkt,
    ss, rs, rs25, rs26, rs27, ls, ws, wr, os, orr, hs, hr,
):
    r, c = lax.axis_index("row"), lax.axis_index("col")
    yl, z, k = r // 8, (r // 2) % 4, r % 2
    yh, x = c // 4, c % 4
    zr, zl, z2 = (z + 1) % 4, (z + 3) % 4, (z + 2) % 4

    def at_row(yl_, z_, k_):
        return (yl_ * 8 + z_ * 2 + k_, c)

    def at_col(yh_, x_):
        return (r, yh_ * 4 + x_)

    sib, ypart = at_row(yl, z, 1 - k), at_row(1 - yl, z, k)
    right, left = at_row(yl, zr, k), at_row(yl, zl, k)
    yhp = at_col(1 - yh, x)
    xr, xl, xx = at_col(yh, (x + 1) % 4), at_col(yh, (x + 3) % 4), at_col(yh, (x + 2) % 4)

    def rc(src, dst, send, recv, dev):
        return pltpu.make_async_remote_copy(
            src_ref=src, dst_ref=dst, send_sem=send, recv_sem=recv,
            device_id=dev, device_id_type=MESH,
        )

    def rows(i, size):
        return pl.ds(pl.multiple_of(i * size, size), size)

    def landed(ref, sem):
        pltpu.make_async_copy(ref, ref, sem).wait()

    def msg(n, i):
        own_p = pl.ds(pl.multiple_of(yl * 64 + z * 16, 16), 16)
        left_p = pl.ds(pl.multiple_of(yl * 64 + zl * 16, 16), 16)
        right_p = pl.ds(pl.multiple_of(yl * 64 + zr * 16, 16), 16)
        own_q = pl.ds(pl.multiple_of(z * 32 + yl * 16, 16), 16)
        if i == 0:
            src, dst, dev = pp.at[n], yp.at[n], ypart
        elif i == 1:
            src, dst, dev = s1.at[n, 0, rows(z2, 16)], rzp.at[n, 0], right
        elif i == 2:
            src, dst, dev = s1.at[n, 1, rows(zr, 16)], rzp.at[n, 2], right
        elif i == 3:
            src, dst, dev = s1.at[n, 1, rows(z2, 16)], rzp.at[n, 1], left
        elif i == 4:
            src, dst, dev = s1.at[n, 0, rows(zl, 16)], rzp.at[n, 3], left
        elif i == 5:
            src, dst, dev = szp.at[n, 0], rzp.at[n, 4], right
        elif i == 6:
            src, dst, dev = szp.at[n, 1], rzp.at[n, 5], left
        elif i in (7, 8):
            src = dst = gp.at[n, :, own_p]
            dev = right if i == 7 else left
        elif i == 9:
            src = dst = gp.at[n, 0, left_p]
            dev = right
        elif i == 10:
            src = dst = gp.at[n, 1, right_p]
            dev = left
        elif i == 11:
            src = dst = gp.at[n, 1, rows(yl, 64)]
            dev = ypart
        elif i == 28:
            src = dst = gp.at[n, 0, rows(yl, 64)]
            dev = ypart
        elif i == 12:
            src, dst, dev = syq.at[n], yq.at[n], ypart
        elif i == 13:
            src, dst, dev = pq.at[n, 0, rows(z2, 32)], rzq.at[n, 0], right
        elif i == 14:
            src, dst, dev = pq.at[n, 1, rows(zr, 32)], rzq.at[n, 2], right
        elif i == 15:
            src, dst, dev = pq.at[n, 1, rows(z2, 32)], rzq.at[n, 1], left
        elif i == 16:
            src, dst, dev = pq.at[n, 0, rows(zl, 32)], rzq.at[n, 3], left
        elif i == 17:
            src, dst, dev = szq.at[n, 0], rzq.at[n, 4], right
        elif i == 18:
            src, dst, dev = szq.at[n, 1], rzq.at[n, 5], left
        elif i == 19:
            src = dst = gq.at[n, :, own_q]
            dev = ypart
        elif i in (20, 21):
            src = dst = gq.at[n, :, rows(z, 32)]
            dev = right if i == 20 else left
        elif i == 22:
            src = dst = gq.at[n, 0, rows(zl, 32)]
            dev = right
        elif i == 23:
            src = dst = gq.at[n, 1, rows(zr, 32)]
            dev = left
        elif i == 24:
            src, dst, dev = doth.at[n], dsib.at[n], sib
        elif i == 27:
            src = dst = tk.at[n, :, :, own_d]
            dev = sib
        if i == 27:
            recv = rs27.at[n]
        else:
            recv = rs.at[n, RECV[i]]
        return rc(src, dst, ss.at[n], recv, dev)

    own_d = pl.ds(pl.multiple_of(k * DH, DH), DH)
    oth_d = pl.ds(pl.multiple_of((1 - k) * DH, DH), DH)
    own_f = pl.ds(pl.multiple_of(k * FH, FH), FH)
    oth_f = pl.ds(pl.multiple_of((1 - k) * FH, FH), FH)

    top, bottom = pl.ds(0, 64), pl.ds(64, 64)

    def tok_msgs(m):
        if m in (1, 2):
            src = tk.at[0, :, (top, bottom)[m - 1], own_d]
            parts = ((src, tk.at[m, :, top, own_d], xl), (src, tk.at[m, :, bottom, own_d], xr))
        else:
            dev = {3: xx, 4: xx, 5: xl, 6: xr, 7: yhp}[m]
            parts = ((tk.at[0 if m in (3, 7) else 7, :, :, own_d], tk.at[m, :, :, own_d], dev),)
        return [rc(src, dst, ss.at[N + 1], rs26.at[m], dev) for src, dst, dev in parts]

    def send_tokens(m):
        for cp in tok_msgs(m):
            cp.start()

    def tokens_landed(m):
        landed(tk.at[m, :, :, own_d], rs26.at[m])

    def send_width(m):
        if m in (1, 2):
            there = (top, bottom)[m - 1]
            parts = ((down.at[m, top], dr.at[1, there], xr), (down.at[m, bottom], dr.at[2, there], xl))
        else:
            parts = ((down.at[m], dr.at[m], {3: xx, 4: xx, 5: xr, 6: xl}[m]),)
        for src, dst, dev in parts:
            rc(src, dst, ss.at[N], rs25.at[(m - 1) // 3], dev).start()

    barrier = pltpu.get_barrier_semaphore()
    partners = (sib, ypart, right, left, yhp, xr, xl, xx)
    for dev in partners:
        pl.semaphore_signal(barrier, inc=1, device_id=dev, device_id_type=MESH)

    w_own, w_out = [], []
    for i, (j, size) in enumerate(TILES):
        mine = pl.ds(pl.multiple_of(k * FH + j, 128), size)
        other = pl.ds(pl.multiple_of((1 - k) * FH + j, 128), size)
        here = pl.ds(j, size)
        w_own += [
            pltpu.make_async_copy(win_ref.at[:, mine], wi.at[own_d, here], ls.at[2 * i]),
            pltpu.make_async_copy(wout_ref.at[mine], wo.at[here, own_d], ls.at[2 * i + 1]),
        ]
        w_out += [
            rc(win_ref.at[:, other], wi.at[own_d, here], ws.at[2 * i], wr.at[2 * i], sib),
            rc(wout_ref.at[other], wo.at[here, own_d], ws.at[2 * i + 1], wr.at[2 * i + 1], sib),
        ]
    w_order = (2, 3, 4, 5, 0, 1)
    for i in w_order:
        w_own[i].start()
    t_own = [
        pltpu.make_async_copy(ref, tk.at[0, i, :, own_d], ls.at[12 + i])
        for i, ref in enumerate((tok_ref, up_ref))
    ]
    for cp in t_own:
        cp.start()
    pl.semaphore_wait(barrier, len(partners))
    for cp in t_own:
        cp.wait()

    msg(0, 27).start()
    send_tokens(1)
    send_tokens(7)
    for i in w_order:
        w_out[i].start()
    send_tokens(2)

    def weights(n, tile):
        @pl.when(n == 0)
        def _():
            for i in (2 * tile, 2 * tile + 1):
                w_own[i].wait()
                w_out[i].wait_recv()

    def zero(n):
        @pl.when(n == 2)
        def _():
            acci[...] = jnp.zeros_like(acci)
            acco[...] = jnp.zeros_like(acco)

    def total(*refs):
        out = refs[0].astype(F32)
        for ref in refs[1:]:
            out = out + ref.astype(F32)
        return out

    def start(n, *copies):
        for i in copies:
            msg(n, i).start()

    def arrived(n, *copies):
        for i in copies:
            msg(n, i).wait_recv()

    def p0(n):
        weights(n, 0)
        ppf[0] = dot(tk[n, 0], wi[:, 0:FP])
        ppf[1] = dot_nt(tk[n, 1], wo[0:FP, :])
        pp[n] = ppf[:, rows(1 - yl, 64)].astype(BF)
        start(n, 0)
        ppo[n] = ppf[:, rows(yl, 64)]

    def q0(n):
        arrived(n, 27)
        for i, (j, size) in enumerate(QT):
            weights(n, 1 + i)
            pq[n, 0, :, j : j + size] = dot(tk[n, 0], wi[:, FP + j : FP + j + size]).astype(BF)
            pq[n, 1, :, j : j + size] = dot_nt(tk[n, 1], wo[FP + j : FP + j + size, :]).astype(BF)
        start(n, 13, 15, 14, 16)

    def p1(n):
        arrived(n, 0)
        s1[n] = total(ppo[n], yp[n]).astype(BF)
        start(n, 1, 3, 2, 4)

    def q1a(n):
        arrived(n, 13)
        szq[n, 0] = total(pq[n, 0, rows(zr, 32)], rzq[n, 0]).astype(BF)
        start(n, 17)

    def q1b(n):
        arrived(n, 15)
        szq[n, 1] = total(pq[n, 1, rows(zl, 32)], rzq[n, 1]).astype(BF)
        start(n, 18)

    def p2a(n):
        arrived(n, 1)
        szp[n, 0] = total(ppo[n, 0, rows(zr, 16)], yp[n, 0, rows(zr, 16)], rzp[n, 0]).astype(BF)
        start(n, 5)

    def p2b(n):
        arrived(n, 3)
        szp[n, 1] = total(ppo[n, 1, rows(zl, 16)], yp[n, 1, rows(zl, 16)], rzp[n, 1]).astype(BF)
        start(n, 6)

    def q2(n):
        landed(rzq.at[n, pl.ds(2, 4)], rs.at[n, RECV[14]])
        for t, a, b in ((0, 3, 4), (1, 2, 5)):
            for mine in (False, True):
                half = yl if mine else 1 - yl
                here = pl.ds(pl.multiple_of(z * 32 + half * 16, 16), 16)
                sums = total(pq[n, t, here], rzq[n, a, rows(half, 16)], rzq[n, b, rows(half, 16)])
                if mine:
                    kq[n, t] = sums
                else:
                    syq[n, t] = sums.astype(BF)
        start(n, 12)

    def p3(n):
        landed(rzp.at[n, pl.ds(2, 4)], rs.at[n, RECV[2]])
        hidden = total(ppo[n, 0, rows(z, 16)], yp[n, 0, rows(z, 16)], rzp[n, 3], rzp[n, 4])
        back = total(ppo[n, 1, rows(z, 16)], yp[n, 1, rows(z, 16)], rzp[n, 2], rzp[n, 5])
        here = pl.ds(pl.multiple_of(yl * 64 + z * 16, 16), 16)
        gp[n, 0, here], gp[n, 1, here] = activate(hidden, back)
        start(n, 7, 8)

    def q3(n):
        arrived(n, 12)
        here = pl.ds(pl.multiple_of(z * 32 + yl * 16, 16), 16)
        gq[n, 0, here], gq[n, 1, here] = activate(total(kq[n, 0], yq[n, 0]), total(kq[n, 1], yq[n, 1]))
        start(n, 19)

    def p4a(n):
        arrived(n, 7)
        start(n, 9)

    def p4b(n):
        arrived(n, 8)
        start(n, 10)

    def q4(n):
        arrived(n, 19)
        start(n, 20, 21)

    def p5(n):
        landed(gp.at[n, :, pl.ds(pl.multiple_of(yl * 64 + z2 * 16, 16), 16)], rs.at[n, RECV[9]])
        start(n, 11, 28)

    def q5a(n):
        arrived(n, 20)
        start(n, 22)

    def q5b(n):
        arrived(n, 21)
        start(n, 23)

    def cols(t, n):
        yield 0, FP, gp[n, t]
        for j, size in QT:
            yield FP + j, size, gq[n, t, :, j : j + size]

    def grads(n):
        landed(gq.at[n, :, rows(z2, 32)], rs.at[n, RECV[22]])
        arrived(n, 11, 28)
        for half, ref in ((oth_d, doth), (own_d, down)):
            ref[n] = dot_nt(gp[n, 1], wi[half, 0:FP]) + dot_nt(gq[n, 1], wi[half, FP:FH])
            if ref is doth:
                start(n, 24)
        tkt[...] = tk[n, 0].T
        for j, size, g in cols(1, n):
            acci[:, j : j + size] += dot(tkt[...], g)
        for j, size, a in cols(0, n):
            acco[j : j + size, :] += dot(a.T, tk[n, 1])

    def s7(n):
        arrived(n, 24)
        down[n] += dsib[n]

    def width_sums(n):
        s7(n)
        for m in range(1, 6):

            @pl.when(n == m)
            def _():
                send_width(m)

    def tokens_in(n):
        for m in range(1, 7):

            @pl.when(n == m - 1)
            def _():
                tokens_landed(m)
                start(m, 27)
                if m == 1:
                    send_tokens(3)
                if m == 2:
                    tokens_landed(7)
                    for far in (4, 5, 6):
                        send_tokens(far)
                    start(7, 27)

    order = (
        (q0, 0), (p0, 0), (q1b, 1), (q2, 3), (p1, 2), (p4a, 5), (p3, 4), (p4b, 5), (p2b, 3),
        (q1a, 1), (q3, 4), (tokens_in, 0), (p2a, 3), (p5, 6), (q4, 5), (zero, 0), (width_sums, 9), (grads, 8), (q5a, 6), (q5b, 6),
    )

    def step(n, _):
        for op, late in order:

            @pl.when((n >= late) & (n < N + late))
            def _():
                op(n - late)

        return 0

    lax.fori_loop(0, N + 7, step, 0)

    last = N - 1
    outs = []

    def give(src, dst, i):
        outs.append(rc(src, dst, os.at[i], orr.at[i], sib))
        outs[-1].start()

    def in_tile(i):
        j, size = TILES[i]
        g = gp[last, 1] if i == 0 else gq[last, 1, :, j - FP : j - FP + size]
        there = pl.ds(pl.multiple_of(k * FH + j, 128), size)
        sti[:, j : j + size] = (acci[oth_d, j : j + size] + dot(tkt[oth_d, :], g)).astype(BF)
        give(sti.at[:, j : j + size], gin_ref.at[:, there], i)
        gin_ref[:, there] = (acci[own_d, j : j + size] + dot(tkt[own_d, :], g)).astype(BF)

    def out_tile(i):
        j, size = TILES[i]
        a = gp[last, 0] if i == 0 else gq[last, 0, :, j - FP : j - FP + size]
        there = pl.ds(pl.multiple_of(k * FH + j, 128), size)
        at = a.T
        sto[j : j + size] = (acco[j : j + size, oth_d] + dot(at, tk[last, 1, :, oth_d])).astype(BF)
        give(sto.at[j : j + size], gout_ref.at[there], 3 + i)
        gout_ref[there] = (acco[j : j + size, own_d] + dot(at, tk[last, 1, :, own_d])).astype(BF)

    s7(last - 1)
    send_width(last - 1)
    tkt[...] = tk[last, 0].T
    landed(gq.at[last, :, rows(z2, 32)], rs.at[last, RECV[22]])
    for half, ref in ((oth_d, doth), (own_d, down)):
        ref[last] = dot_nt(gq[last, 1], wi[half, FP:FH])
    for i in (1, 2):
        in_tile(i)
        out_tile(i)
    arrived(last, 11)
    for half, ref in ((oth_d, doth), (own_d, down)):
        ref[last] += dot_nt(gp[last, 1], wi[half, 0:FP])
        if ref is doth:
            start(last, 24)
    in_tile(0)
    s7(last)
    landed(dr.at[pl.ds(4, 3)], rs25.at[1])
    yhs[...] = (down[last] + dr[4] + dr[5] + dr[6]).astype(BF)
    yh_msg = rc(yhs, yhr, hs.at[0], hr.at[0], yhp)
    yh_msg.start()
    arrived(last, 28)
    out_tile(0)
    landed(dr.at[pl.ds(1, 3)], rs25.at[0])
    yh_msg.wait()
    gtok_ref[...] = (down[0] + dr[1] + dr[2] + dr[3] + yhr[...].astype(F32)).astype(BF)
    for cp in outs:
        cp.wait()

    for n in range(N):
        landed(wo.at[pl.ds(0, 1152)], ss.at[n])
    landed(wo.at[pl.ds(0, 768)], ss.at[N])
    landed(wo.at[pl.ds(0, 896)], ss.at[N + 1])
    for cp in w_out:
        cp.wait_send()


def hand_on(gtok, gin, gout, gtok_out, gin_out, gout_out, sem):
    copies = [
        pltpu.make_async_copy(a, b, sem.at[i])
        for i, (a, b) in enumerate(((gin, gin_out), (gout, gout_out), (gtok, gtok_out)))
    ]
    for cp in copies:
        cp.start()
    for cp in copies:
        cp.wait()


def shards(tokens, weight_in, weight_out, upstream):
    vm = lambda *shape, dtype=BF: pltpu.VMEM(shape, dtype)
    dma = lambda *shape: pltpu.SemaphoreType.DMA(shape)
    vmem, hbm = pl.BlockSpec(memory_space=pltpu.VMEM), pl.BlockSpec(memory_space=pl.ANY)
    results = pl.pallas_call(
        kernel,
        out_shape=(
            vm(TB, DH),
            vm(DH, 2 * FH),
            vm(2 * FH, DH),
        ),
        in_specs=[hbm] * 4,
        out_specs=(vmem, vmem, vmem),
        scratch_shapes=[
            vm(DC, FH), vm(FH, DC), vm(N, 2, TB, DC),
            vm(2, TB, FP, dtype=F32), vm(N, 2, 64, FP, dtype=F32), vm(N, 2, 64, FP), vm(N, 2, 64, FP), vm(N, 2, 64, FP), vm(N, 6, 16, FP), vm(N, 2, 16, FP), vm(N, 2, TB, FP),
            vm(N, 2, TB, FQ), vm(N, 6, 32, FQ), vm(N, 2, 32, FQ), vm(N, 2, 16, FQ, dtype=F32), vm(N, 2, 16, FQ), vm(N, 2, 16, FQ), vm(N, 2, TB, FQ),
            vm(DC, FH, dtype=F32), vm(FH, DC, dtype=F32), vm(DH, FH), vm(FH, DH),
            vm(N, TB, DH, dtype=F32), vm(N, TB, DH, dtype=F32), vm(N, TB, DH, dtype=F32), vm(N, TB, DH, dtype=F32),
            vm(TB, DH), vm(TB, DH), vm(DC, TB),
            dma(N + 2), dma(N, 18), dma(2), dma(N), dma(N), dma(14), dma(6), dma(6), dma(6), dma(6), dma(1), dma(1),
        ],
        compiler_params=pltpu.CompilerParams(
            collective_id=0, has_side_effects=True, vmem_limit_bytes=53 << 20
        ),
    )(tokens, weight_in, weight_out, upstream)
    return pl.pallas_call(
        hand_on,
        out_shape=tuple(jax.ShapeDtypeStruct(a.shape, a.dtype) for a in results),
        in_specs=[vmem] * 3,
        out_specs=(hbm,) * 3,
        scratch_shapes=[dma(3)],
        compiler_params=pltpu.CompilerParams(vmem_limit_bytes=1 << 20),
    )(*(pltpu.with_memory_space_constraint(a, pltpu.VMEM) for a in results))


def solution(mesh):
    placed = (P("col", "row"), P("row", "col"), P("col", "row"), P("col", "row"))
    return jax.shard_map(
        shards,
        mesh=mesh,
        in_specs=placed,
        out_specs=(P("col", "row"), P("row", "col"), P("col", "row")),
        check_vma=False,
    )
```

```python
import jax
import jax.numpy as jnp
from jax import lax
from jax.experimental import pallas as pl
from jax.experimental.pallas import tpu as pltpu
from jax.sharding import PartitionSpec as P

coef = 0.7978845608
cubic = 0.044715
BF = jnp.bfloat16
F32 = jnp.float32
MESH = pl.DeviceIdType.MESH

N = 8
TB = 128
DH = 384
DC = 768
FH = 1536
FP = 640
FQ = 896
RECV = {0: 0, 1: 1, 3: 2, 2: 3, 4: 3, 5: 3, 6: 3, 7: 4, 8: 5, 9: 6, 10: 6, 11: 7}
RECV |= {13: 8, 15: 9, 14: 10, 16: 10, 17: 10, 18: 10, 12: 11, 19: 12, 20: 13, 21: 14, 22: 15, 23: 15, 24: 16, 28: 17, 29: 15, 30: 15, 31: 6, 32: 6}
QT = ((0, 512), (512, FQ - 512))
TILES = ((0, FP),) + tuple((FP + j, size) for j, size in QT)


def activate(hidden, back):
    inner = coef * (hidden + cubic * hidden * hidden * hidden)
    tangent = jnp.tanh(inner)
    value = 0.5 * hidden * (1.0 + tangent)
    slope = 0.5 * (1.0 + tangent) + 0.5 * hidden * (1.0 - tangent * tangent) * coef * (
        1.0 + 3.0 * cubic * hidden * hidden
    )
    return value.astype(BF), (back * slope).astype(BF)


def dot(left, right):
    return jnp.dot(left, right, preferred_element_type=F32)


def dot_nt(left, right):
    return lax.dot_general(
        left, right, (((1,), (1,)), ((), ())), preferred_element_type=F32
    )


def kernel(
    tok_ref, win_ref, wout_ref, up_ref,
    gtok_ref, gin_ref, gout_ref,
    wi, wo, tk, ppf, ppo, pp, yp, s1, rzp, szp, gp, pq, rzq, szq, kq, syq, yq, gq,
    acci, acco, sti, sto, down, doth, dsib, dr, yhs, yhr, tkt,
    ss, rs, rs25, rs26, rs27, ls, ws, wr, os, orr, hs, hr,
):
    r, c = lax.axis_index("row"), lax.axis_index("col")
    yl, z, k = r // 8, (r // 2) % 4, r % 2
    yh, x = c // 4, c % 4
    zr, zl, z2 = (z + 1) % 4, (z + 3) % 4, (z + 2) % 4

    def at_row(yl_, z_, k_):
        return (yl_ * 8 + z_ * 2 + k_, c)

    def at_col(yh_, x_):
        return (r, yh_ * 4 + x_)

    sib, ypart = at_row(yl, z, 1 - k), at_row(1 - yl, z, k)
    right, left = at_row(yl, zr, k), at_row(yl, zl, k)
    yhp = at_col(1 - yh, x)
    xr, xl, xx = at_col(yh, (x + 1) % 4), at_col(yh, (x + 3) % 4), at_col(yh, (x + 2) % 4)

    def rc(src, dst, send, recv, dev):
        return pltpu.make_async_remote_copy(
            src_ref=src, dst_ref=dst, send_sem=send, recv_sem=recv,
            device_id=dev, device_id_type=MESH,
        )

    def rows(i, size):
        return pl.ds(pl.multiple_of(i * size, size), size)

    def landed(ref, sem):
        pltpu.make_async_copy(ref, ref, sem).wait()

    def msg(n, i):
        own_p = pl.ds(pl.multiple_of(yl * 64 + z * 16, 16), 16)
        left_p = pl.ds(pl.multiple_of(yl * 64 + zl * 16, 16), 16)
        right_p = pl.ds(pl.multiple_of(yl * 64 + zr * 16, 16), 16)
        own_q = pl.ds(pl.multiple_of(z * 32 + yl * 16, 16), 16)
        if i == 0:
            src, dst, dev = pp.at[n], yp.at[n], ypart
        elif i == 1:
            src, dst, dev = s1.at[n, 0, rows(z2, 16)], rzp.at[n, 0], right
        elif i == 2:
            src, dst, dev = s1.at[n, 1, rows(zr, 16)], rzp.at[n, 2], right
        elif i == 3:
            src, dst, dev = s1.at[n, 1, rows(z2, 16)], rzp.at[n, 1], left
        elif i == 4:
            src, dst, dev = s1.at[n, 0, rows(zl, 16)], rzp.at[n, 3], left
        elif i == 5:
            src, dst, dev = szp.at[n, 0], rzp.at[n, 4], right
        elif i == 6:
            src, dst, dev = szp.at[n, 1], rzp.at[n, 5], left
        elif i in (7, 8, 31, 32):
            src = dst = gp.at[n, 0 if i in (7, 32) else 1, own_p]
            dev = right if i in (7, 31) else left
        elif i == 9:
            src = dst = gp.at[n, 0, left_p]
            dev = right
        elif i == 10:
            src = dst = gp.at[n, 1, right_p]
            dev = left
        elif i == 11:
            src = dst = gp.at[n, 1, rows(yl, 64)]
            dev = ypart
        elif i == 28:
            src = dst = gp.at[n, 0, rows(yl, 64)]
            dev = ypart
        elif i == 12:
            src, dst, dev = syq.at[n], yq.at[n], ypart
        elif i == 13:
            src, dst, dev = pq.at[n, 0, rows(z2, 32)], rzq.at[n, 0], right
        elif i == 14:
            src, dst, dev = pq.at[n, 1, rows(zr, 32)], rzq.at[n, 2], right
        elif i == 15:
            src, dst, dev = pq.at[n, 1, rows(z2, 32)], rzq.at[n, 1], left
        elif i == 16:
            src, dst, dev = pq.at[n, 0, rows(zl, 32)], rzq.at[n, 3], left
        elif i == 17:
            src, dst, dev = szq.at[n, 0], rzq.at[n, 4], right
        elif i == 18:
            src, dst, dev = szq.at[n, 1], rzq.at[n, 5], left
        elif i == 19:
            src = dst = gq.at[n, :, own_q]
            dev = ypart
        elif i in (20, 21, 29, 30):
            src = dst = gq.at[n, 0 if i in (20, 30) else 1, rows(z, 32)]
            dev = right if i in (20, 29) else left
        elif i == 22:
            src = dst = gq.at[n, 0, rows(zl, 32)]
            dev = right
        elif i == 23:
            src = dst = gq.at[n, 1, rows(zr, 32)]
            dev = left
        elif i == 24:
            src, dst, dev = doth.at[n], dsib.at[n], sib
        elif i == 27:
            src = dst = tk.at[n, :, :, own_d]
            dev = sib
        if i == 27:
            recv = rs27.at[n]
        else:
            recv = rs.at[n % 6, RECV[i]]
        return rc(src, dst, ss.at[n], recv, dev)

    own_d = pl.ds(pl.multiple_of(k * DH, DH), DH)
    oth_d = pl.ds(pl.multiple_of((1 - k) * DH, DH), DH)
    own_f = pl.ds(pl.multiple_of(k * FH, FH), FH)
    oth_f = pl.ds(pl.multiple_of((1 - k) * FH, FH), FH)

    top, bottom = pl.ds(0, 64), pl.ds(64, 64)

    def tok_msgs(m):
        if m in (1, 2):
            src = tk.at[0, :, (top, bottom)[m - 1], own_d]
            parts = ((src, tk.at[m, :, top, own_d], xl), (src, tk.at[m, :, bottom, own_d], xr))
        else:
            dev = {3: xx, 4: xx, 5: xl, 6: xr, 7: yhp}[m]
            parts = ((tk.at[0 if m in (3, 7) else 7, :, :, own_d], tk.at[m, :, :, own_d], dev),)
        return [rc(src, dst, ss.at[N + 1], rs26.at[m], dev) for src, dst, dev in parts]

    def send_tokens(m):
        for cp in tok_msgs(m):
            cp.start()

    def tokens_landed(m):
        landed(tk.at[m, :, :, own_d], rs26.at[m])

    def send_width(m):
        if m in (1, 2):
            there = (top, bottom)[m - 1]
            parts = ((down.at[m, top], dr.at[1, there], xr), (down.at[m, bottom], dr.at[2, there], xl))
        else:
            parts = ((down.at[m], dr.at[m], {3: xx, 4: xx, 5: xr, 6: xl}[m]),)
        for src, dst, dev in parts:
            rc(src, dst, ss.at[N], rs25.at[(m - 1) // 3], dev).start()

    barrier = pltpu.get_barrier_semaphore()
    partners = (sib, ypart, right, left, yhp, xr, xl, xx)
    for dev in partners:
        pl.semaphore_signal(barrier, inc=1, device_id=dev, device_id_type=MESH)

    w_own, w_out = [], []
    for i, (j, size) in enumerate(TILES):
        mine = pl.ds(pl.multiple_of(k * FH + j, 128), size)
        other = pl.ds(pl.multiple_of((1 - k) * FH + j, 128), size)
        here = pl.ds(j, size)
        w_own += [
            pltpu.make_async_copy(win_ref.at[:, mine], wi.at[own_d, here], ls.at[2 * i]),
            pltpu.make_async_copy(wout_ref.at[mine], wo.at[here, own_d], ls.at[2 * i + 1]),
        ]
        w_out += [
            rc(win_ref.at[:, other], wi.at[own_d, here], ws.at[2 * i], wr.at[2 * i], sib),
            rc(wout_ref.at[other], wo.at[here, own_d], ws.at[2 * i + 1], wr.at[2 * i + 1], sib),
        ]
    w_order = (2, 3, 4, 5, 0, 1)
    for i in w_order:
        w_own[i].start()
    t_own = [
        pltpu.make_async_copy(ref, tk.at[0, i, :, own_d], ls.at[12 + i])
        for i, ref in enumerate((tok_ref, up_ref))
    ]
    for cp in t_own:
        cp.start()
    pl.semaphore_wait(barrier, len(partners))
    for cp in t_own:
        cp.wait()

    msg(0, 27).start()
    send_tokens(1)
    send_tokens(7)
    for i in w_order:
        w_out[i].start()
    send_tokens(2)

    def weights(n, tile):
        @pl.when(n == 0)
        def _():
            for i in (2 * tile, 2 * tile + 1):
                w_own[i].wait()
                w_out[i].wait_recv()

    def zero(n):
        @pl.when(n == 2)
        def _():
            acci[...] = jnp.zeros_like(acci)
            acco[...] = jnp.zeros_like(acco)

    def total(*refs):
        out = refs[0].astype(F32)
        for ref in refs[1:]:
            out = out + ref.astype(F32)
        return out

    def start(n, *copies):
        for i in copies:
            msg(n, i).start()

    def arrived(n, *copies):
        for i in copies:
            msg(n, i).wait_recv()

    def p0(n):
        weights(n, 0)
        ppf[0] = dot(tk[n, 0], wi[:, 0:FP])
        ppf[1] = dot_nt(tk[n, 1], wo[0:FP, :])
        pp[n] = ppf[:, rows(1 - yl, 64)].astype(BF)
        start(n, 0)
        ppo[n] = ppf[:, rows(yl, 64)]

    def q0(n):
        arrived(n, 27)
        for i, (j, size) in enumerate(QT):
            weights(n, 1 + i)
            pq[n, 0, :, j : j + size] = dot(tk[n, 0], wi[:, FP + j : FP + j + size]).astype(BF)
            pq[n, 1, :, j : j + size] = dot_nt(tk[n, 1], wo[FP + j : FP + j + size, :]).astype(BF)
        start(n, 13, 15, 14, 16)

    def p1(n):
        arrived(n, 0)
        s1[n] = total(ppo[n], yp[n]).astype(BF)
        start(n, 1, 3, 2, 4)

    def q1a(n):
        arrived(n, 13)
        szq[n, 0] = total(pq[n, 0, rows(zr, 32)], rzq[n, 0]).astype(BF)
        start(n, 17)

    def q1b(n):
        arrived(n, 15)
        szq[n, 1] = total(pq[n, 1, rows(zl, 32)], rzq[n, 1]).astype(BF)
        start(n, 18)

    def p2a(n):
        arrived(n, 1)
        szp[n, 0] = total(ppo[n, 0, rows(zr, 16)], yp[n, 0, rows(zr, 16)], rzp[n, 0]).astype(BF)
        start(n, 5)

    def p2b(n):
        arrived(n, 3)
        szp[n, 1] = total(ppo[n, 1, rows(zl, 16)], yp[n, 1, rows(zl, 16)], rzp[n, 1]).astype(BF)
        start(n, 6)

    def q2(n):
        landed(rzq.at[n, pl.ds(2, 4)], rs.at[n % 6, RECV[14]])
        for t, a, b in ((0, 3, 4), (1, 2, 5)):
            for mine in (False, True):
                half = yl if mine else 1 - yl
                here = pl.ds(pl.multiple_of(z * 32 + half * 16, 16), 16)
                sums = total(pq[n, t, here], rzq[n, a, rows(half, 16)], rzq[n, b, rows(half, 16)])
                if mine:
                    kq[n, t] = sums
                else:
                    syq[n, t] = sums.astype(BF)
        start(n, 12)

    def p3(n):
        landed(rzp.at[n, pl.ds(2, 4)], rs.at[n % 6, RECV[2]])
        hidden = total(ppo[n, 0, rows(z, 16)], yp[n, 0, rows(z, 16)], rzp[n, 3], rzp[n, 4])
        back = total(ppo[n, 1, rows(z, 16)], yp[n, 1, rows(z, 16)], rzp[n, 2], rzp[n, 5])
        here = pl.ds(pl.multiple_of(yl * 64 + z * 16, 16), 16)
        gp[n, 0, here], gp[n, 1, here] = activate(hidden, back)
        start(n, 7, 8, 31, 32)

    def q3(n):
        arrived(n, 12)
        here = pl.ds(pl.multiple_of(z * 32 + yl * 16, 16), 16)
        gq[n, 0, here], gq[n, 1, here] = activate(total(kq[n, 0], yq[n, 0]), total(kq[n, 1], yq[n, 1]))
        start(n, 19)

    def p4a(n):
        arrived(n, 7)
        start(n, 9)

    def p4b(n):
        arrived(n, 8)
        start(n, 10)

    def q4(n):
        arrived(n, 19)
        start(n, 20, 21, 29, 30)

    def p5(n):
        landed(rzp.at[n, pl.ds(0, 4)], rs.at[n % 6, RECV[9]])
        start(n, 11, 28)

    def q5a(n):
        arrived(n, 20)
        start(n, 22)

    def q5b(n):
        arrived(n, 21)
        start(n, 23)

    def cols(t, n):
        yield 0, FP, gp[n, t]
        for j, size in QT:
            yield FP + j, size, gq[n, t, :, j : j + size]

    def grads(n):
        landed(rzq.at[n, pl.ds(0, 4)], rs.at[n % 6, RECV[22]])
        arrived(n, 11, 28)
        for half, ref in ((oth_d, doth), (own_d, down)):
            ref[n] = dot_nt(gp[n, 1], wi[half, 0:FP]) + dot_nt(gq[n, 1], wi[half, FP:FH])
            if ref is doth:
                start(n, 24)
        tkt[...] = tk[n, 0].T
        for j, size, g in cols(1, n):
            acci[:, j : j + size] += dot(tkt[...], g)
        for j, size, a in cols(0, n):
            acco[j : j + size, :] += dot(a.T, tk[n, 1])

    def s7(n):
        arrived(n, 24)
        down[n] += dsib[n]

    def width_sums(n):
        s7(n)
        for m in range(1, 6):

            @pl.when(n == m)
            def _():
                send_width(m)

    def tokens_in(n):
        for m in range(1, 7):

            @pl.when(n == m - 1)
            def _():
                tokens_landed(m)
                start(m, 27)
                if m == 1:
                    send_tokens(3)
                if m == 2:
                    tokens_landed(7)
                    for far in (4, 5, 6):
                        send_tokens(far)
                    start(7, 27)

    order = (
        (q0, 0), (p0, 0), (q1b, 1), (q2, 3), (p1, 2), (p4a, 5), (p3, 4), (p4b, 5), (p2b, 3),
        (q1a, 1), (q3, 4), (tokens_in, 0), (p2a, 3), (p5, 6), (q4, 5), (q5a, 6), (q5b, 6), (zero, 0), (width_sums, 8), (grads, 7),
    )

    def step(n, _):
        for op, late in order:

            @pl.when((n >= late) & (n < N + late))
            def _():
                op(n - late)

        return 0

    lax.fori_loop(0, N + 6, step, 0)

    last = N - 1
    outs = []

    def give(src, dst, i):
        outs.append(rc(src, dst, os.at[i], orr.at[i], sib))
        outs[-1].start()

    def in_tile(i):
        j, size = TILES[i]
        g = gp[last, 1] if i == 0 else gq[last, 1, :, j - FP : j - FP + size]
        there = pl.ds(pl.multiple_of(k * FH + j, 128), size)
        sti[:, j : j + size] = (acci[oth_d, j : j + size] + dot(tkt[oth_d, :], g)).astype(BF)
        give(sti.at[:, j : j + size], gin_ref.at[:, there], i)
        gin_ref[:, there] = (acci[own_d, j : j + size] + dot(tkt[own_d, :], g)).astype(BF)

    def out_tile(i):
        j, size = TILES[i]
        a = gp[last, 0] if i == 0 else gq[last, 0, :, j - FP : j - FP + size]
        there = pl.ds(pl.multiple_of(k * FH + j, 128), size)
        at = a.T
        sto[j : j + size] = (acco[j : j + size, oth_d] + dot(at, tk[last, 1, :, oth_d])).astype(BF)
        give(sto.at[j : j + size], gout_ref.at[there], 3 + i)
        gout_ref[there] = (acco[j : j + size, own_d] + dot(at, tk[last, 1, :, own_d])).astype(BF)

    s7(last - 1)
    send_width(last - 1)
    tkt[...] = tk[last, 0].T
    landed(rzq.at[last, pl.ds(0, 4)], rs.at[last % 6, RECV[22]])
    for half, ref in ((oth_d, doth), (own_d, down)):
        ref[last] = dot_nt(gq[last, 1], wi[half, FP:FH])
    arrived(last, 11)
    for half, ref in ((oth_d, doth), (own_d, down)):
        ref[last] += dot_nt(gp[last, 1], wi[half, 0:FP])
        if ref is doth:
            start(last, 24)
    in_tile(1)
    s7(last)
    landed(dr.at[pl.ds(4, 3)], rs25.at[1])
    yhs[...] = (down[last] + dr[4] + dr[5] + dr[6]).astype(BF)
    yh_msg = rc(yhs, yhr, hs.at[0], hr.at[0], yhp)
    yh_msg.start()
    in_tile(2)
    in_tile(0)
    out_tile(1)
    out_tile(2)
    arrived(last, 28)
    out_tile(0)
    landed(dr.at[pl.ds(1, 3)], rs25.at[0])
    yh_msg.wait()
    gtok_ref[...] = (down[0] + dr[1] + dr[2] + dr[3] + yhr[...].astype(F32)).astype(BF)
    for cp in outs:
        cp.wait()

    for n in range(N):
        landed(wo.at[pl.ds(0, 1152)], ss.at[n])
    landed(wo.at[pl.ds(0, 768)], ss.at[N])
    landed(wo.at[pl.ds(0, 896)], ss.at[N + 1])
    for cp in w_out:
        cp.wait_send()


def hand_on(gtok, gin, gout, gtok_out, gin_out, gout_out, sem):
    copies = [
        pltpu.make_async_copy(a, b, sem.at[i])
        for i, (a, b) in enumerate(((gin, gin_out), (gout, gout_out), (gtok, gtok_out)))
    ]
    for cp in copies:
        cp.start()
    for cp in copies:
        cp.wait()


def shards(tokens, weight_in, weight_out, upstream):
    vm = lambda *shape, dtype=BF: pltpu.VMEM(shape, dtype)
    dma = lambda *shape: pltpu.SemaphoreType.DMA(shape)
    vmem, hbm = pl.BlockSpec(memory_space=pltpu.VMEM), pl.BlockSpec(memory_space=pl.ANY)
    results = pl.pallas_call(
        kernel,
        out_shape=(
            vm(TB, DH),
            vm(DH, 2 * FH),
            vm(2 * FH, DH),
        ),
        in_specs=[hbm] * 4,
        out_specs=(vmem, vmem, vmem),
        scratch_shapes=[
            vm(DC, FH), vm(FH, DC), vm(N, 2, TB, DC),
            vm(2, TB, FP, dtype=F32), vm(N, 2, 64, FP, dtype=F32), vm(N, 2, 64, FP), vm(N, 2, 64, FP), vm(N, 2, 64, FP), vm(N, 6, 16, FP), vm(N, 2, 16, FP), vm(N, 2, TB, FP),
            vm(N, 2, TB, FQ), vm(N, 6, 32, FQ), vm(N, 2, 32, FQ), vm(N, 2, 16, FQ, dtype=F32), vm(N, 2, 16, FQ), vm(N, 2, 16, FQ), vm(N, 2, TB, FQ),
            vm(DC, FH, dtype=F32), vm(FH, DC, dtype=F32), vm(DH, FH), vm(FH, DH),
            vm(N, TB, DH, dtype=F32), vm(N, TB, DH, dtype=F32), vm(N, TB, DH, dtype=F32), vm(N, TB, DH, dtype=F32),
            vm(TB, DH), vm(TB, DH), vm(DC, TB),
            dma(N + 2), dma(6, 18), dma(2), dma(N), dma(N), dma(14), dma(6), dma(6), dma(6), dma(6), dma(1), dma(1),
        ],
        compiler_params=pltpu.CompilerParams(
            collective_id=0, has_side_effects=True, vmem_limit_bytes=53 << 20
        ),
    )(tokens, weight_in, weight_out, upstream)
    return pl.pallas_call(
        hand_on,
        out_shape=tuple(jax.ShapeDtypeStruct(a.shape, a.dtype) for a in results),
        in_specs=[vmem] * 3,
        out_specs=(hbm,) * 3,
        scratch_shapes=[dma(3)],
        compiler_params=pltpu.CompilerParams(vmem_limit_bytes=1 << 20),
    )(*(pltpu.with_memory_space_constraint(a, pltpu.VMEM) for a in results))


def solution(mesh):
    placed = (P("col", "row"), P("row", "col"), P("col", "row"), P("col", "row"))
    return jax.shard_map(
        shards,
        mesh=mesh,
        in_specs=placed,
        out_specs=(P("col", "row"), P("row", "col"), P("col", "row")),
        check_vma=False,
    )
```
